256 devices in a mesh: tm: 16 (over z_hi, y), sx: 4 (over z_lo, core), sy: 4 (over x).
Axes of the slice: x: 4, y: 4, z: 8 (z_hi: 4, z_lo: 2; z = z_hi * 2 + z_lo), core: 2. Of those that a mesh axis runs over, the one named last changes fastest.
Arguments:
- start: float32 [32, 128, 256], P('sx', 'sy'), may hold values from -6 to 6
- guess: float32 [16, 32, 128, 256], P('tm', 'sx', 'sy'), may hold values from -10 to 10
- forcing: float32 [64, 32, 128, 256], P('tm', 'sx', 'sy'), may hold values from -8 to 8
- absorb: float32 [32, 128, 256], P('sx', 'sy'), may hold values from 0.004 to 0.25
Outputs:
- solution: float32 [64, 32, 128, 256], P('tm', 'sx', 'sy')
The draws below stay inside these ranges and needn't reach their ends.
All inputs are finite; a program needn't handle non-finite values.
Results may differ from the reference program's by a relative error of at most 0.00006.
Values sent between devices are 32-bit elements; how exact they have to be, the bound alone decides.
No kernel may reach another device: no remote copies, remote signals or barrier semaphores. Data moves between devices by JAX's collectives and lax.ppermute only.
A program may use at most 64 MiB of HBM per device.

```python
import math
import jax
import jax.numpy as jnp

NZ = 256
STEPS_DEV = 4
SWEEPS = 4
COARSE_SWEEPS = 2
NX = 32
NY = 128
COARSE = 16
NT = 64
N_TM = 16


WAVES = ((1, 1, 1), (2, 1, 1), (1, 2, 1), (1, 1, 2), (2, 2, 1), (1, 3, 2))


def profile(cells, wave):
    place = (jnp.arange(cells, dtype=jnp.float32) + 0.5) / cells
    return jnp.sin(math.pi * wave * place)


def shape_of(wave):
    return profile(NX, wave[0])[:, None, None] * profile(NY, wave[1])[None, :, None] * profile(NZ, wave[2])[None, None, :]


def smooth_sum(weights, rough):
    total = rough
    for index in range(len(WAVES)):
        total = total + weights[:, index, None, None, None] * shape_of(WAVES[index])[None]
    return total


def draw_guess(key, part):
    key = jax.random.fold_in(key, 11)
    weight_key, rough_key = jax.random.split(key)
    weights = 0.5 * jax.random.truncated_normal(weight_key, -2.0, 2.0, (COARSE, len(WAVES)), jnp.float32)
    rough = jax.random.truncated_normal(rough_key, -4.0, 4.0, (COARSE, NX, NY, NZ), jnp.float32)
    return smooth_sum(weights, rough)


def draw_forcing(key, part):
    key = jax.random.fold_in(key, 23)
    weight_key, rough_key = jax.random.split(key, 2)
    weights = 0.25 * jax.random.truncated_normal(weight_key, -2.0, 2.0, (NT, len(WAVES)), jnp.float32)
    rough = jax.random.truncated_normal(rough_key, -4.0, 4.0, (NT, NX, NY, NZ), jnp.float32)
    return smooth_sum(weights, rough)


def block_scale(own_key, extent, cuts, low, largest):
    factor_of = 1.0
    for dim, parts in cuts:
        draws = jax.random.uniform(jax.random.fold_in(jax.random.fold_in(own_key, 6), dim), (parts,), jnp.float32, low / len(cuts), largest / len(cuts))
        factor_of = factor_of * jnp.repeat(jnp.exp(draws), extent[dim] // parts).reshape((-1,) + (1,) * (len(extent) - 1 - dim))
    return factor_of


def gaussian(own_key, shape, scale, most, cuts=(), held_as=jnp.bfloat16):
    drawn = scale * jax.random.normal(own_key, shape, jnp.float32)
    if cuts:
        drawn = drawn * block_scale(own_key, shape, cuts, -0.22, 0.18)
    return jnp.clip(drawn, -most, most).astype(held_as)


def setup_inputs(seed: int = 0) -> dict:
    key_of = jax.random.split(jax.random.key(seed), 5)
    start = gaussian(key_of[0], (NX, NY, NZ), 1.0, 6.0, ((0, 4), (1, 4)), jnp.float32)
    guess = draw_guess(jax.random.fold_in(key_of[4], 71), 0)
    forcing = draw_forcing(jax.random.fold_in(key_of[4], 71), 0)
    absorb = jnp.clip(jnp.exp(math.log(0.25) - 4.1351665 * jax.random.uniform(key_of[3], (NX, NY, NZ), jnp.float32) ** block_scale(key_of[3], (NX, NY, NZ), ((0, 4), (1, 4)), -0.2, 0.2)), 0.004, 0.25)
    return dict(start=start, guess=guess, forcing=forcing, absorb=absorb)


DIFFUSION = 0.5
DRIFT_X = 0.5
DRIFT_Y = 0.3
DRIFT_Z = 0.2


def relax(first, rhs, absorb, scale, sweeps):
    coupling = DIFFUSION * scale
    lean_x = DRIFT_X * scale
    lean_y = DRIFT_Y * scale
    lean_z = DRIFT_Z * scale
    diag = 1.0 + 6.0 * coupling + lean_x + lean_y + lean_z + scale * absorb
    value = first
    lead = [(0, 0)] * (value.ndim - 3)
    for sweep in range(sweeps):
        padded = jnp.pad(value, lead + [(1, 1), (1, 1), (1, 1)])
        low_x = padded[..., :-2, 1:-1, 1:-1]
        low_y = padded[..., 1:-1, :-2, 1:-1]
        low_z = padded[..., 1:-1, 1:-1, :-2]
        beside_all = low_x + padded[..., 2:, 1:-1, 1:-1] + low_y + padded[..., 1:-1, 2:, 1:-1]
        beside_all = beside_all + low_z + padded[..., 1:-1, 1:-1, 2:]
        value = (rhs + coupling * beside_all + lean_x * low_x + lean_y * low_y + lean_z * low_z) / diag
    return value


def advance(value, source, absorb):
    return relax(value, value + source, absorb, 1.0, SWEEPS)


def coarse_step(value, absorb):
    return relax(value, value, absorb, float(STEPS_DEV), COARSE_SWEEPS)


def reference(start, guess, forcing, absorb):
    blocks = forcing.reshape(N_TM, STEPS_DEV, NX, NY, NZ)
    before = jnp.concatenate([start[None], guess[:-1]], axis=0)
    state = before
    for inner in range(STEPS_DEV - 1):
        state = advance(state, blocks[:, inner], absorb)
    resid = advance(state, blocks[:, STEPS_DEV - 1], absorb) - guess
    error = jnp.zeros((NX, NY, NZ), jnp.float32)
    errors = []
    for index in range(N_TM):
        error = coarse_step(error, absorb) + resid[index]
        errors.append(error)
    corrected = guess + jnp.stack(errors, axis=0)
    state = jnp.concatenate([start[None], corrected[:-1]], axis=0)
    pieces = []
    for inner in range(STEPS_DEV - 1):
        state = advance(state, blocks[:, inner], absorb)
        pieces.append(state)
    pieces.append(corrected)
    return jnp.stack(pieces, axis=1).reshape(NT, NX, NY, NZ)
```

```python
import functools
import jax
import jax.numpy as jnp
from jax import lax
from jax.experimental import pallas as pl
from jax.experimental.pallas import tpu as pltpu
from jax.sharding import PartitionSpec as P

NX = 32
ROWS = 8
NZ = 256
EXT = 3 * ROWS
PART = 64
MARGIN = 32
WINDOW = PART + 2 * MARGIN
GROUP = 4
F32 = jnp.float32
WX = 2.0
WY = 1.6
WZ = 1.4


def device_of(block):
    sy, local = divmod(block % 16, 4)
    return (local ^ (2 * (sy & 1))) * 4 + sy


def block_swap(first):
    pairs = []
    for block in range(16):
        other = block + 1 if (block - first) % 2 == 0 else block - 1
        pairs.append((device_of(block), device_of(other % 16)))
    return pairs


IN_CHIP = block_swap(0)
OFF_CHIP = block_swap(1)


def both_sides(value):
    axes = ("sx", "sy")
    return lax.ppermute(value, axes, IN_CHIP), lax.ppermute(value, axes, OFF_CHIP)


def sweep(source, target, hinv, rhs, closed):
    width = source.shape[2]
    rows = source.shape[1]
    lane = lax.broadcasted_iota(jnp.int32, (rows, width), 1)

    def body(x, carry):
        here = source[x + 1]
        low_z = pltpu.roll(here, 1, 1)
        high_z = pltpu.roll(here, width - 1, 1)
        if closed:
            low_z = jnp.where(lane == 0, 0.0, low_z)
            high_z = jnp.where(lane == width - 1, 0.0, high_z)
        low_y = pltpu.roll(here, 1, 0)
        high_y = pltpu.roll(here, rows - 1, 0)
        total = (source[x + 2] + WX * source[x]) + (high_y + WY * low_y) + (high_z + WZ * low_z)
        target[x + 1] = (total + rhs(x, here)) * hinv[x]
        return carry

    lax.fori_loop(0, NX, body, 0, unroll=4)


def clear_ends(*states):
    for state in states:
        blank = jnp.zeros(state.shape[1:], F32)
        state[0] = blank
        state[NX + 1] = blank


def joined(flags, centre, in_chip, off_chip):
    low = in_chip * flags[0] + off_chip * flags[1]
    high = in_chip * flags[2] + off_chip * flags[3]
    return jnp.concatenate([low, centre, high], axis=0)


def each_x(body):
    def step(x, carry):
        body(x)
        return carry

    lax.fori_loop(0, NX, step, 0, unroll=2)


def relax(a, b, hinv, saved, sweeps, closed, scale, extra=None):
    def first(x, here):
        value = scale * here if extra is None else scale * (here + extra(x))
        saved[x] = value
        return value

    sweep(a, b, hinv, first, closed)
    for index in range(1, sweeps):
        source, target = (b, a) if index % 2 else (a, b)
        sweep(source, target, hinv, lambda x, here: saved[x], closed)


def centre_of(value):
    return value[ROWS : 2 * ROWS]


def begin_kernel(flags, x_c, x_i, x_o, s_c, s_i, s_o, place, w1, w2, fine, coarse, window, a, b, saved):
    fl = [flags[k] for k in range(4)]
    shift = place[0]
    lane = lax.broadcasted_iota(jnp.int32, (EXT, WINDOW), 1) + place[1]
    inside = jnp.logical_and(lane >= 0, lane < NZ)
    row = lax.broadcasted_iota(jnp.int32, (EXT, NZ), 0) + place[2]
    real = jnp.logical_and(row >= 0, row < 16 * ROWS)
    clear_ends(a, b)

    def fill(x):
        hi, lo = x // 8, x % 8
        a[x + 1] = joined(fl, x_c[x], x_i[x], x_o[x])
        absorb = joined(fl, s_c[hi, 0, lo], s_i[hi, 0, lo], s_o[hi, 0, lo])
        fine[x] = jnp.where(real, 0.5 / (5.0 + absorb), 0.0)
        value = jnp.where(real, 2.0 / (17.0 + 4.0 * absorb), 0.0)
        coarse[x] = value
        window[x] = jnp.where(inside, pltpu.roll(value, shift, 1)[:, :WINDOW], 0.0)

    each_x(fill)

    def source(index):
        def get(x):
            hi, lo = x // 8, x % 8
            return joined(fl, s_c[hi, index, lo], s_i[hi, index, lo], s_o[hi, index, lo])

        return get

    for index, out in ((1, w1), (2, w2)):
        relax(a, b, fine, saved, 4, True, 2.0, source(index))

        def put(x):
            out[x] = centre_of(a[x + 1])

        each_x(put)


def resid_kernel(flags, v_c, v_i, v_o, s_c, s_i, s_o, own, fine, w3, resid, chunks, a, b, saved):
    fl = [flags[k] for k in range(4)]
    clear_ends(a, b)

    def fill(x):
        a[x + 1] = joined(fl, v_c[x], v_i[x], v_o[x])

    each_x(fill)

    def source(index):
        def get(x):
            hi, lo = x // 8, x % 8
            return joined(fl, s_c[hi, index, lo], s_i[hi, index, lo], s_o[hi, index, lo])

        return get

    relax(a, b, fine, saved, 4, True, 2.0, source(0))

    def put(x):
        w3[x] = centre_of(a[x + 1])

    each_x(put)
    relax(a, b, fine, saved, 4, True, 2.0, source(1))
    lane = lax.broadcasted_iota(jnp.int32, (ROWS, WINDOW), 1)

    def split(x):
        value = centre_of(a[x + 1]) - own[x // 8, x % 8]
        resid[x] = value
        for part in range(GROUP):
            start = PART * part - MARGIN
            turned = pltpu.roll(value, (-start) % NZ, 1)[:, :WINDOW]
            if part == 0:
                turned = jnp.where(lane < MARGIN, 0.0, turned)
            if part == GROUP - 1:
                turned = jnp.where(lane >= WINDOW - MARGIN, 0.0, turned)
            chunks[part, x] = turned

    each_x(split)


def chain_kernel(first, last, flags, r_c, r_i, r_o, hinv, *refs):
    if first:
        out, a, b, saved = refs
    else:
        e_c, e_i, e_o, out, a, b, saved = refs
    fl = [flags[k] for k in range(4)]
    clear_ends(a, b)
    lane = lax.broadcasted_iota(jnp.int32, (ROWS, WINDOW), 1)

    def added(step, x):
        if step < GROUP - 1:
            return joined(fl, r_c[step, x], r_i[step, x], r_o[step, x])
        blank = jnp.zeros((ROWS, WINDOW), F32)
        return jnp.concatenate([blank, r_c[step, x], blank], axis=0)

    def fill(x):
        if first:
            a[x + 1] = added(0, x)
        else:
            gate = flags[4]
            a[x + 1] = gate * joined(fl, e_c[x], e_i[x], e_o[x])

    each_x(fill)

    def pack(step):
        def put(x, carry):
            low = pltpu.roll(centre_of(a[x + 1]), WINDOW - MARGIN, 1)
            high = pltpu.roll(centre_of(a[x + 1 + NX // 2]), MARGIN, 1)
            out[step, x] = jnp.where(lane < PART, low, high)
            return carry

        lax.fori_loop(0, NX // 2, put, 0, unroll=2)

    for step in range(1 if first else 0, GROUP):
        if last:
            pack(step)
            if step == GROUP - 1:
                return
        relax(a, b, hinv, saved, 2, False, 0.5)

        def add(x):
            a[x + 1] = a[x + 1] + added(step, x)

        each_x(add)

    def put_all(x):
        out[x] = centre_of(a[x + 1])

    each_x(put_all)


def unpacked(packed, x, lane):
    p = [packed[part, x] for part in range(GROUP)]
    low = lane < PART
    first = jnp.concatenate(
        [jnp.where(low, p[0], pltpu.roll(p[1], PART, 1)), jnp.where(low, p[2], pltpu.roll(p[3], PART, 1))],
        axis=1,
    )
    second = jnp.concatenate(
        [jnp.where(low, pltpu.roll(p[0], PART, 1), p[1]), jnp.where(low, pltpu.roll(p[2], PART, 1), p[3])],
        axis=1,
    )
    return first, second


def correct_kernel(
    flags, d_c, d_i, d_o, fine, coarse, own, resid, w1, w2, out, y2, a, b, saved, kept
):
    fl = [flags[k] for k in range(4)]
    clear_ends(a, b)
    lane = lax.broadcasted_iota(jnp.int32, (ROWS, WINDOW), 1)
    half = NX // 2

    def fill(x, carry):
        for index, values in enumerate(
            zip(unpacked(d_c, x, lane), unpacked(d_i, x, lane), unpacked(d_o, x, lane))
        ):
            value = joined(fl, *values)
            a[x + half * index + 1] = value
            kept[x + half * index] = value
        return carry

    lax.fori_loop(0, half, fill, 0)
    relax(a, b, coarse, saved, 2, True, 0.5)

    def put(x):
        hi, lo = x // 8, x % 8
        out[hi, 2, lo] = (centre_of(a[x + 1]) + resid[x]) + own[hi, lo]
        a[x + 1] = kept[x]

    each_x(put)
    for index, base in enumerate((w1, w2)):
        relax(a, b, fine, saved, 4, True, 2.0)

        def place(x):
            value = centre_of(a[x + 1])
            out[x // 8, index, x % 8] = value + base[x]
            if index == 1:
                y2[x] = value

        each_x(place)


def end_kernel(flags, y_c, y_i, y_o, fine, w3, out, a, b, saved):
    fl = [flags[k] for k in range(4)]
    clear_ends(a, b)

    def fill(x):
        a[x + 1] = joined(fl, y_c[x], y_i[x], y_o[x])

    each_x(fill)
    relax(a, b, fine, saved, 4, True, 2.0)

    def put(x):
        out[x // 8, x % 8] = centre_of(a[x + 1]) + w3[x]

    each_x(put)


def call(kernel, outs, width, args, smem, kept=False):
    scratch = [
        pltpu.VMEM((NX + 2, EXT, width), F32),
        pltpu.VMEM((NX + 2, EXT, width), F32),
        pltpu.VMEM((NX, EXT, width), F32),
    ]
    if kept:
        scratch.append(pltpu.VMEM((NX, EXT, width), F32))
    specs = [
        pl.BlockSpec(memory_space=pltpu.SMEM if index in smem else pltpu.VMEM)
        for index in range(len(args))
    ]
    return pl.pallas_call(
        kernel,
        out_shape=[jax.ShapeDtypeStruct(shape, F32) for shape in outs],
        in_specs=specs,
        out_specs=[pl.BlockSpec(memory_space=pltpu.VMEM)] * len(outs),
        scratch_shapes=scratch,
        compiler_params=pltpu.CompilerParams(vmem_limit_bytes=48 * 2**20),
    )(*args)


def on_device(start, guess, forcing, absorb):
    tm = lax.axis_index("tm")
    sx = lax.axis_index("sx")
    sy = lax.axis_index("sy")
    turned = sy % 2 == 1
    local = jnp.where(turned, (sx + 2) % 4, sx)
    block = 4 * sy + local
    even = block % 2 == 0
    inner_low = jnp.logical_not(even)
    outer_low = jnp.logical_and(even, block > 0)
    inner_high = even
    outer_high = jnp.logical_and(jnp.logical_not(even), block < 15)
    gate = tm >= GROUP
    flags = jnp.stack([inner_low, outer_low, inner_high, outer_high, gate]).astype(F32)
    part = tm % GROUP
    place = jnp.stack([(MARGIN - PART * part) % NZ, PART * part - MARGIN, ROWS * block - ROWS])
    place = place.astype(jnp.int32)

    def to_blocks(fields):
        count = fields.shape[0]
        cut = fields.reshape(count, 8, 4, ROWS, NZ)
        cut = jnp.where(turned, jnp.roll(cut, 2, axis=2), cut)
        return lax.all_to_all(jnp.moveaxis(cut, 2, 0), "sx", 0, 0)

    own = guess[0]
    shifted = lax.ppermute(own, "tm", [(c, (c + 1) % 16) for c in range(16)])
    early = to_blocks(jnp.stack([absorb, forcing[0], forcing[1]]))
    early_i, early_o = both_sides(early)
    before = to_blocks(jnp.where(tm == 0, start, shifted)[None]).reshape(NX, ROWS, NZ)
    before_i, before_o = both_sides(before)
    late = to_blocks(jnp.concatenate([forcing[2:4], guess], axis=0))
    late_f = late[:, :2]
    late_i, late_o = both_sides(late_f)
    guess_b = late[:, 2]

    field = (NX, ROWS, NZ)
    w1, w2, fine, coarse, window = call(
        begin_kernel,
        [field, field, (NX, EXT, NZ), (NX, EXT, NZ), (NX, EXT, WINDOW)],
        NZ,
        (flags, before, before_i, before_o, early, early_i, early_o, place),
        (0, 7),
    )
    w2_i, w2_o = both_sides(w2)
    w3, resid, chunks = call(
        resid_kernel,
        [field, field, (GROUP, NX, ROWS, WINDOW)],
        NZ,
        (flags, w2, w2_i, w2_o, late_f, late_i, late_o, guess_b, fine),
        (0,),
    )
    groups = [[GROUP * g + j for j in range(GROUP)] for g in range(4)]
    held = lax.all_to_all(chunks, "tm", 0, 0, axis_index_groups=groups)
    held_i, held_o = both_sides(held[: GROUP - 1])
    plane = (NX, ROWS, WINDOW)
    (state,) = call(
        functools.partial(chain_kernel, True, False), [plane], WINDOW,
        (flags, held, held_i, held_o, window), (0,),
    )
    for turn in range(3):
        state = lax.ppermute(state, "tm", [(c, (c + GROUP) % 16) for c in range(16)])
        state_i, state_o = both_sides(state)
        last = turn == 2
        (state,) = call(
            functools.partial(chain_kernel, False, last),
            [(GROUP, NX // 2, ROWS, WINDOW) if last else plane], WINDOW,
            (flags, held, held_i, held_o, window, state, state_i, state_o), (0,),
        )
    error = lax.all_to_all(state, "tm", 0, 0, axis_index_groups=groups)
    error_i, error_o = both_sides(error)
    out, y2 = call(
        correct_kernel,
        [(4, 3, 8, ROWS, NZ), field],
        NZ,
        (flags, error, error_i, error_o, fine, coarse, guess_b, resid, w1, w2),
        (0,),
        kept=True,
    )
    y2_i, y2_o = both_sides(y2)
    (last,) = call(
        end_kernel, [(4, 8, ROWS, NZ)], NZ, (flags, y2, y2_i, y2_o, fine, w3), (0,)
    )
    fields = jnp.stack([out[:, 0], out[:, 1], last, out[:, 2]], axis=1)
    back = lax.all_to_all(fields, "sx", 0, 0)
    back = jnp.where(turned, jnp.roll(back, 2, axis=0), back)
    return jnp.moveaxis(back, 0, 2).reshape(4, 8, 4 * ROWS, NZ)


def solution(mesh):
    placed = (
        P("sx", "sy", None),
        P("tm", "sx", "sy", None),
        P("tm", "sx", "sy", None),
        P("sx", "sy", None),
    )
    return jax.shard_map(
        on_device, mesh=mesh, in_specs=placed, out_specs=P("tm", "sx", "sy", None), check_vma=False
    )
```

```python
import functools
import jax
import jax.numpy as jnp
from jax import lax
from jax.experimental import pallas as pl
from jax.experimental.pallas import tpu as pltpu
from jax.sharding import PartitionSpec as P

NX = 32
ROWS = 8
NZ = 256
EXT = 3 * ROWS
PART = 64
MARGIN = 32
WINDOW = PART + 2 * MARGIN
GROUP = 4
F32 = jnp.float32
WX = 2.0
WY = 1.6
WZ = 1.4


def device_of(block):
    sy, local = divmod(block % 16, 4)
    return (local ^ (2 * (sy & 1))) * 4 + sy


def block_swap(first):
    pairs = []
    for block in range(16):
        other = block + 1 if (block - first) % 2 == 0 else block - 1
        pairs.append((device_of(block), device_of(other % 16)))
    return pairs


IN_CHIP = block_swap(0)
OFF_CHIP = block_swap(1)


def both_sides(value):
    axes = ("sx", "sy")
    return lax.ppermute(value, axes, IN_CHIP), lax.ppermute(value, axes, OFF_CHIP)


def sweep(source, target, hinv, saved, closed):
    width = source.shape[2]
    rows = source.shape[1]
    lane = lax.broadcasted_iota(jnp.int32, (rows, width), 1)

    def body(x, carry):
        here = source[x + 1]
        low_z = pltpu.roll(here, 1, 1)
        high_z = pltpu.roll(here, width - 1, 1)
        if closed:
            low_z = jnp.where(lane == 0, 0.0, low_z)
            high_z = jnp.where(lane == width - 1, 0.0, high_z)
        low_y = pltpu.roll(here, 1, 0)
        high_y = pltpu.roll(here, rows - 1, 0)
        total = (source[x + 2] + WX * source[x]) + (high_y + WY * low_y) + (high_z + WZ * low_z)
        target[x + 1] = (total + saved[x]) * hinv[x]
        return carry

    lax.fori_loop(0, NX, body, 0, unroll=True)


def clear_ends(*states):
    for state in states:
        blank = jnp.zeros(state.shape[1:], F32)
        state[0] = blank
        state[NX + 1] = blank


def joined(flags, centre, in_chip, off_chip):
    low = in_chip * flags[0] + off_chip * flags[1]
    high = in_chip * flags[2] + off_chip * flags[3]
    return jnp.concatenate([low, centre, high], axis=0)


def each_x(body):
    def step(x, carry):
        body(x)
        return carry

    lax.fori_loop(0, NX, step, 0, unroll=8)


def relax(a, b, hinv, saved, pairs, closed):
    def pair(index, carry):
        sweep(a, b, hinv, saved, closed)
        sweep(b, a, hinv, saved, closed)
        return carry

    lax.fori_loop(0, pairs, pair, 0)


def centre_of(value):
    return value[ROWS : 2 * ROWS]


def begin_kernel(flags, x_c, x_i, x_o, s_c, s_i, s_o, place, w1, w2, fine, coarse, window, a, b, saved):
    fl = [flags[k] for k in range(4)]
    shift = place[0]
    lane = lax.broadcasted_iota(jnp.int32, (EXT, WINDOW), 1) + place[1]
    inside = jnp.logical_and(lane >= 0, lane < NZ)
    row = lax.broadcasted_iota(jnp.int32, (EXT, NZ), 0) + place[2]
    real = jnp.logical_and(row >= 0, row < 16 * ROWS)
    clear_ends(a, b)

    def source(index, x):
        hi, lo = x // 8, x % 8
        return joined(fl, s_c[hi, index, lo], s_i[hi, index, lo], s_o[hi, index, lo])

    def fill(x):
        hi, lo = x // 8, x % 8
        value = joined(fl, x_c[x], x_i[x], x_o[x])
        a[x + 1] = value
        saved[x] = 2.0 * (value + source(1, x))
        absorb = joined(fl, s_c[hi, 0, lo], s_i[hi, 0, lo], s_o[hi, 0, lo])
        fine[x] = jnp.where(real, 0.5 / (5.0 + absorb), 0.0)
        value = jnp.where(real, 2.0 / (17.0 + 4.0 * absorb), 0.0)
        coarse[x] = value
        window[x] = jnp.where(inside, pltpu.roll(value, shift, 1)[:, :WINDOW], 0.0)

    each_x(fill)
    relax(a, b, fine, saved, 2, True)

    def turn(x):
        value = a[x + 1]
        w1[x] = centre_of(value)
        saved[x] = 2.0 * (value + source(2, x))

    each_x(turn)
    relax(a, b, fine, saved, 2, True)

    def put(x):
        w2[x] = centre_of(a[x + 1])

    each_x(put)


def resid_kernel(flags, v_c, v_i, v_o, s_c, s_i, s_o, own, fine, w3, resid, chunks, a, b, saved):
    fl = [flags[k] for k in range(4)]
    clear_ends(a, b)

    def source(index, x):
        hi, lo = x // 8, x % 8
        return joined(fl, s_c[hi, index, lo], s_i[hi, index, lo], s_o[hi, index, lo])

    def fill(x):
        value = joined(fl, v_c[x], v_i[x], v_o[x])
        a[x + 1] = value
        saved[x] = 2.0 * (value + source(0, x))

    each_x(fill)
    relax(a, b, fine, saved, 2, True)

    def turn(x):
        value = a[x + 1]
        w3[x] = centre_of(value)
        saved[x] = 2.0 * (value + source(1, x))

    each_x(turn)
    relax(a, b, fine, saved, 2, True)
    lane = lax.broadcasted_iota(jnp.int32, (ROWS, WINDOW), 1)

    def split(x):
        value = centre_of(a[x + 1]) - own[x // 8, x % 8]
        resid[x] = value
        for part in range(GROUP):
            start = PART * part - MARGIN
            turned = pltpu.roll(value, (-start) % NZ, 1)[:, :WINDOW]
            if part == 0:
                turned = jnp.where(lane < MARGIN, 0.0, turned)
            if part == GROUP - 1:
                turned = jnp.where(lane >= WINDOW - MARGIN, 0.0, turned)
            chunks[part, x] = turned

    each_x(split)


def chain_kernel(first, last, flags, r_c, r_i, r_o, hinv, *refs):
    if first:
        out, a, b, saved = refs
    else:
        e_c, e_i, e_o, out, a, b, saved = refs
    fl = [flags[k] for k in range(4)]
    clear_ends(a, b)
    lane = lax.broadcasted_iota(jnp.int32, (ROWS, WINDOW), 1)

    def added(step, x):
        if step < GROUP - 1:
            return joined(fl, r_c[step, x], r_i[step, x], r_o[step, x])
        blank = jnp.zeros((ROWS, WINDOW), F32)
        return jnp.concatenate([blank, r_c[step, x], blank], axis=0)

    def fill(x):
        value = added(0, x) if first else flags[4] * joined(fl, e_c[x], e_i[x], e_o[x])
        a[x + 1] = value
        saved[x] = 0.5 * value

    each_x(fill)

    def pack(step):
        def put(x, carry):
            low = pltpu.roll(centre_of(a[x + 1]), WINDOW - MARGIN, 1)
            high = pltpu.roll(centre_of(a[x + 1 + NX // 2]), MARGIN, 1)
            out[step, x] = jnp.where(lane < PART, low, high)
            return carry

        lax.fori_loop(0, NX // 2, put, 0, unroll=8)

    for step in range(1 if first else 0, GROUP):
        if last:
            pack(step)
            if step == GROUP - 1:
                return
        relax(a, b, hinv, saved, 1, False)

        def add(x):
            value = a[x + 1] + added(step, x)
            a[x + 1] = value
            saved[x] = 0.5 * value

        each_x(add)

    def put_all(x):
        out[x] = centre_of(a[x + 1])

    each_x(put_all)


def unpacked(packed, x, lane):
    p = [packed[part, x] for part in range(GROUP)]
    low = lane < PART
    first = jnp.concatenate(
        [jnp.where(low, p[0], pltpu.roll(p[1], PART, 1)), jnp.where(low, p[2], pltpu.roll(p[3], PART, 1))],
        axis=1,
    )
    second = jnp.concatenate(
        [jnp.where(low, pltpu.roll(p[0], PART, 1), p[1]), jnp.where(low, pltpu.roll(p[2], PART, 1), p[3])],
        axis=1,
    )
    return first, second


def correct_kernel(
    flags, d_c, d_i, d_o, fine, coarse, own, resid, w1, w2, out, y2, a, b, saved, kept
):
    fl = [flags[k] for k in range(4)]
    clear_ends(a, b)
    lane = lax.broadcasted_iota(jnp.int32, (ROWS, WINDOW), 1)
    half = NX // 2

    def fill(x, carry):
        for index, values in enumerate(
            zip(unpacked(d_c, x, lane), unpacked(d_i, x, lane), unpacked(d_o, x, lane))
        ):
            value = joined(fl, *values)
            a[x + half * index + 1] = value
            kept[x + half * index] = value
            saved[x + half * index] = 0.5 * value
        return carry

    lax.fori_loop(0, half, fill, 0, unroll=4)
    relax(a, b, coarse, saved, 1, True)

    def put(x):
        hi, lo = x // 8, x % 8
        out[hi, 2, lo] = (centre_of(a[x + 1]) + resid[x]) + own[hi, lo]
        value = kept[x]
        a[x + 1] = value
        saved[x] = 2.0 * value

    each_x(put)
    for index, base in enumerate((w1, w2)):
        relax(a, b, fine, saved, 2, True)

        def place(x):
            value = centre_of(a[x + 1])
            out[x // 8, index, x % 8] = value + base[x]
            if index == 1:
                y2[x] = value
            else:
                saved[x] = 2.0 * a[x + 1]

        each_x(place)


def end_kernel(flags, y_c, y_i, y_o, fine, w3, out, a, b, saved):
    fl = [flags[k] for k in range(4)]
    clear_ends(a, b)

    def fill(x):
        value = joined(fl, y_c[x], y_i[x], y_o[x])
        a[x + 1] = value
        saved[x] = 2.0 * value

    each_x(fill)
    relax(a, b, fine, saved, 2, True)

    def put(x):
        out[x // 8, x % 8] = centre_of(a[x + 1]) + w3[x]

    each_x(put)


def call(kernel, outs, width, args, smem, kept=False):
    scratch = [
        pltpu.VMEM((NX + 2, EXT, width), F32),
        pltpu.VMEM((NX + 2, EXT, width), F32),
        pltpu.VMEM((NX, EXT, width), F32),
    ]
    if kept:
        scratch.append(pltpu.VMEM((NX, EXT, width), F32))
    specs = [
        pl.BlockSpec(memory_space=pltpu.SMEM if index in smem else pltpu.VMEM)
        for index in range(len(args))
    ]
    return pl.pallas_call(
        kernel,
        out_shape=[jax.ShapeDtypeStruct(shape, F32) for shape in outs],
        in_specs=specs,
        out_specs=[pl.BlockSpec(memory_space=pltpu.VMEM)] * len(outs),
        scratch_shapes=scratch,
        compiler_params=pltpu.CompilerParams(vmem_limit_bytes=48 * 2**20),
    )(*args)


def on_device(start, guess, forcing, absorb):
    tm = lax.axis_index("tm")
    sx = lax.axis_index("sx")
    sy = lax.axis_index("sy")
    turned = sy % 2 == 1
    local = jnp.where(turned, (sx + 2) % 4, sx)
    block = 4 * sy + local
    even = block % 2 == 0
    inner_low = jnp.logical_not(even)
    outer_low = jnp.logical_and(even, block > 0)
    inner_high = even
    outer_high = jnp.logical_and(jnp.logical_not(even), block < 15)
    gate = tm >= GROUP
    flags = jnp.stack([inner_low, outer_low, inner_high, outer_high, gate]).astype(F32)
    part = tm % GROUP
    place = jnp.stack([(MARGIN - PART * part) % NZ, PART * part - MARGIN, ROWS * block - ROWS])
    place = place.astype(jnp.int32)

    def to_blocks(fields):
        count = fields.shape[0]
        cut = fields.reshape(count, 8, 4, ROWS, NZ)
        cut = jnp.where(turned, jnp.roll(cut, 2, axis=2), cut)
        return lax.all_to_all(jnp.moveaxis(cut, 2, 0), "sx", 0, 0)

    own = guess[0]
    shifted = lax.ppermute(own, "tm", [(c, (c + 1) % 16) for c in range(16)])
    early = to_blocks(jnp.stack([absorb, forcing[0], forcing[1]]))
    early_i, early_o = both_sides(early)
    before = to_blocks(jnp.where(tm == 0, start, shifted)[None]).reshape(NX, ROWS, NZ)
    before_i, before_o = both_sides(before)
    late = to_blocks(jnp.concatenate([forcing[2:4], guess], axis=0))
    late_f = late[:, :2]
    late_i, late_o = both_sides(late_f)
    guess_b = late[:, 2]

    field = (NX, ROWS, NZ)
    w1, w2, fine, coarse, window = call(
        begin_kernel,
        [field, field, (NX, EXT, NZ), (NX, EXT, NZ), (NX, EXT, WINDOW)],
        NZ,
        (flags, before, before_i, before_o, early, early_i, early_o, place),
        (0, 7),
    )
    w2_i, w2_o = both_sides(w2)
    w3, resid, chunks = call(
        resid_kernel,
        [field, field, (GROUP, NX, ROWS, WINDOW)],
        NZ,
        (flags, w2, w2_i, w2_o, late_f, late_i, late_o, guess_b, fine),
        (0,),
    )
    groups = [[GROUP * g + j for j in range(GROUP)] for g in range(4)]
    held = lax.all_to_all(chunks, "tm", 0, 0, axis_index_groups=groups)
    held_i, held_o = both_sides(held[: GROUP - 1])
    plane = (NX, ROWS, WINDOW)
    (state,) = call(
        functools.partial(chain_kernel, True, False), [plane], WINDOW,
        (flags, held, held_i, held_o, window), (0,),
    )
    for turn in range(3):
        state = lax.ppermute(state, "tm", [(c, (c + GROUP) % 16) for c in range(16)])
        state_i, state_o = both_sides(state)
        last = turn == 2
        (state,) = call(
            functools.partial(chain_kernel, False, last),
            [(GROUP, NX // 2, ROWS, WINDOW) if last else plane], WINDOW,
            (flags, held, held_i, held_o, window, state, state_i, state_o), (0,),
        )
    error = lax.all_to_all(state, "tm", 0, 0, axis_index_groups=groups)
    error_i, error_o = both_sides(error)
    out, y2 = call(
        correct_kernel,
        [(4, 3, 8, ROWS, NZ), field],
        NZ,
        (flags, error, error_i, error_o, fine, coarse, guess_b, resid, w1, w2),
        (0,),
        kept=True,
    )
    y2_i, y2_o = both_sides(y2)
    (last,) = call(
        end_kernel, [(4, 8, ROWS, NZ)], NZ, (flags, y2, y2_i, y2_o, fine, w3), (0,)
    )
    fields = jnp.stack([out[:, 0], out[:, 1], last, out[:, 2]], axis=1)
    back = lax.all_to_all(fields, "sx", 0, 0)
    back = jnp.where(turned, jnp.roll(back, 2, axis=0), back)
    return jnp.moveaxis(back, 0, 2).reshape(4, 8, 4 * ROWS, NZ)


def solution(mesh):
    placed = (
        P("sx", "sy", None),
        P("tm", "sx", "sy", None),
        P("tm", "sx", "sy", None),
        P("sx", "sy", None),
    )
    return jax.shard_map(
        on_device, mesh=mesh, in_specs=placed, out_specs=P("tm", "sx", "sy", None), check_vma=False
    )
```

```python
import functools
import jax
import jax.numpy as jnp
from jax import lax
from jax.experimental import pallas as pl
from jax.experimental.pallas import tpu as pltpu
from jax.sharding import PartitionSpec as P

NX = 32
ROWS = 8
NZ = 256
EXT = 3 * ROWS
PART = 64
MARGIN = 32
WINDOW = PART + 2 * MARGIN
GROUP = 4
F32 = jnp.float32
WX = 2.0
WY = 1.6
WZ = 1.4


def device_of(block):
    sy, local = divmod(block % 16, 4)
    return (local ^ (2 * (sy & 1))) * 4 + sy


def block_swap(first):
    pairs = []
    for block in range(16):
        other = block + 1 if (block - first) % 2 == 0 else block - 1
        pairs.append((device_of(block), device_of(other % 16)))
    return pairs


IN_CHIP = block_swap(0)
OFF_CHIP = block_swap(1)


def both_sides(value):
    axes = ("sx", "sy")
    return lax.ppermute(value, axes, IN_CHIP), lax.ppermute(value, axes, OFF_CHIP)


def sweep(source, target, hinv, saved, closed):
    width = source.shape[2]
    rows = source.shape[1]
    lane = lax.broadcasted_iota(jnp.int32, (rows, width), 1)

    def body(x, carry):
        here = source[x + 1]
        low_z = pltpu.roll(here, 1, 1)
        high_z = pltpu.roll(here, width - 1, 1)
        if closed:
            low_z = jnp.where(lane == 0, 0.0, low_z)
            high_z = jnp.where(lane == width - 1, 0.0, high_z)
        low_y = pltpu.roll(here, 1, 0)
        high_y = pltpu.roll(here, rows - 1, 0)
        total = (source[x + 2] + WX * source[x]) + (high_y + WY * low_y) + (high_z + WZ * low_z)
        target[x + 1] = (total + saved[x]) * hinv[x]
        return carry

    lax.fori_loop(0, NX, body, 0, unroll=True)


def clear_ends(*states):
    for state in states:
        blank = jnp.zeros(state.shape[1:], F32)
        state[0] = blank
        state[NX + 1] = blank


def joined(flags, centre, in_chip, off_chip):
    low = in_chip * flags[0] + off_chip * flags[1]
    high = in_chip * flags[2] + off_chip * flags[3]
    return jnp.concatenate([low, centre, high], axis=0)


def each_x(body):
    def step(x, carry):
        body(x)
        return carry

    lax.fori_loop(0, NX, step, 0, unroll=8)


def relax(a, b, hinv, saved, pairs, closed):
    def pair(index, carry):
        sweep(a, b, hinv, saved, closed)
        sweep(b, a, hinv, saved, closed)
        return carry

    lax.fori_loop(0, pairs, pair, 0)


def centre_of(value):
    return value[ROWS : 2 * ROWS]


def begin_kernel(flags, s_c, s_i, s_o, place, w1, w2, fine, coarse, window, a, b, saved):
    fl = [flags[k] for k in range(4)]
    shift = place[0]
    lane = lax.broadcasted_iota(jnp.int32, (EXT, WINDOW), 1) + place[1]
    inside = jnp.logical_and(lane >= 0, lane < NZ)
    row = lax.broadcasted_iota(jnp.int32, (EXT, NZ), 0) + place[2]
    real = jnp.logical_and(row >= 0, row < 16 * ROWS)
    clear_ends(a, b)

    def source(index, x):
        return joined(fl, s_c[index, x], s_i[index, x], s_o[index, x])

    def fill(x):
        value = source(3, x)
        a[x + 1] = value
        saved[x] = 2.0 * (value + source(1, x))
        absorb = source(0, x)
        fine[x] = jnp.where(real, 0.5 / (5.0 + absorb), 0.0)
        value = jnp.where(real, 2.0 / (17.0 + 4.0 * absorb), 0.0)
        coarse[x] = value
        window[x] = jnp.where(inside, pltpu.roll(value, shift, 1)[:, :WINDOW], 0.0)

    each_x(fill)
    relax(a, b, fine, saved, 2, True)

    def turn(x):
        value = a[x + 1]
        w1[x] = centre_of(value)
        saved[x] = 2.0 * (value + source(2, x))

    each_x(turn)
    relax(a, b, fine, saved, 2, True)

    def put(x):
        w2[x] = centre_of(a[x + 1])

    each_x(put)


def resid_kernel(flags, v_c, v_i, v_o, s_c, s_i, s_o, own, fine, w3, resid, chunks, a, b, saved):
    fl = [flags[k] for k in range(4)]
    clear_ends(a, b)

    def source(index, x):
        return joined(fl, s_c[index, x], s_i[index, x], s_o[index, x])

    def fill(x):
        value = joined(fl, v_c[x], v_i[x], v_o[x])
        a[x + 1] = value
        saved[x] = 2.0 * (value + source(0, x))

    each_x(fill)
    relax(a, b, fine, saved, 2, True)

    def turn(x):
        value = a[x + 1]
        w3[x] = centre_of(value)
        saved[x] = 2.0 * (value + source(1, x))

    each_x(turn)
    relax(a, b, fine, saved, 2, True)
    lane = lax.broadcasted_iota(jnp.int32, (ROWS, WINDOW), 1)

    def split(x):
        value = centre_of(a[x + 1]) - own[x]
        resid[x] = value
        for part in range(GROUP):
            start = PART * part - MARGIN
            turned = pltpu.roll(value, (-start) % NZ, 1)[:, :WINDOW]
            if part == 0:
                turned = jnp.where(lane < MARGIN, 0.0, turned)
            if part == GROUP - 1:
                turned = jnp.where(lane >= WINDOW - MARGIN, 0.0, turned)
            chunks[part, x] = turned

    each_x(split)


def chain_kernel(first, last, flags, r_c, r_i, r_o, hinv, *refs):
    if first:
        out, a, b, saved = refs
    else:
        e_c, e_i, e_o, out, a, b, saved = refs
    fl = [flags[k] for k in range(4)]
    clear_ends(a, b)
    lane = lax.broadcasted_iota(jnp.int32, (ROWS, WINDOW), 1)

    def added(step, x):
        if step < GROUP - 1:
            return joined(fl, r_c[step, x], r_i[step, x], r_o[step, x])
        blank = jnp.zeros((ROWS, WINDOW), F32)
        return jnp.concatenate([blank, r_c[step, x], blank], axis=0)

    def fill(x):
        value = added(0, x) if first else flags[4] * joined(fl, e_c[x], e_i[x], e_o[x])
        a[x + 1] = value
        saved[x] = 0.5 * value

    each_x(fill)

    def pack(step):
        def put(x, carry):
            low = pltpu.roll(centre_of(a[x + 1]), WINDOW - MARGIN, 1)
            high = pltpu.roll(centre_of(a[x + 1 + NX // 2]), MARGIN, 1)
            out[step, x] = jnp.where(lane < PART, low, high)
            return carry

        lax.fori_loop(0, NX // 2, put, 0, unroll=8)

    for step in range(1 if first else 0, GROUP):
        if last:
            pack(step)
            if step == GROUP - 1:
                return
        relax(a, b, hinv, saved, 1, False)

        def add(x):
            value = a[x + 1] + added(step, x)
            a[x + 1] = value
            saved[x] = 0.5 * value

        each_x(add)

    def put_all(x):
        out[x] = centre_of(a[x + 1])

    each_x(put_all)


def power_kernel(flags, e_c, e_i, e_o, hinv, out, a, b, saved):
    fl = [flags[k] for k in range(4)]
    clear_ends(a, b)

    def fill(x):
        value = joined(fl, e_c[x], e_i[x], e_o[x])
        a[x + 1] = value
        saved[x] = 0.5 * value

    each_x(fill)
    for step in range(GROUP):
        relax(a, b, hinv, saved, 1, False)
        if step < GROUP - 1:

            def again(x):
                saved[x] = 0.5 * a[x + 1]

            each_x(again)

    def put(x):
        out[x] = centre_of(a[x + 1])

    each_x(put)


def unpacked(packed, x, lane):
    p = [packed[part, x] for part in range(GROUP)]
    low = lane < PART
    first = jnp.concatenate(
        [jnp.where(low, p[0], pltpu.roll(p[1], PART, 1)), jnp.where(low, p[2], pltpu.roll(p[3], PART, 1))],
        axis=1,
    )
    second = jnp.concatenate(
        [jnp.where(low, pltpu.roll(p[0], PART, 1), p[1]), jnp.where(low, pltpu.roll(p[2], PART, 1), p[3])],
        axis=1,
    )
    return first, second


def together(copies):
    for copy in copies:
        copy.start()
    for copy in copies:
        copy.wait()


def deal(sx, source, targets, sems):
    together(
        [
            pltpu.make_async_copy(source.at[jnp.bitwise_xor(sx, index)], target, sems.at[index])
            for index, target in enumerate(targets)
        ]
    )


def correct_kernel(
    flags, place, d_c, d_i, d_o, fine, coarse, own, resid, w1, w2,
    out_0, out_1, out_2, out_3, y2, a, b, saved, kept, out, sems,
):
    fl = [flags[k] for k in range(4)]
    clear_ends(a, b)
    lane = lax.broadcasted_iota(jnp.int32, (ROWS, WINDOW), 1)
    half = NX // 2

    def fill(x, carry):
        for index, values in enumerate(
            zip(unpacked(d_c, x, lane), unpacked(d_i, x, lane), unpacked(d_o, x, lane))
        ):
            value = joined(fl, *values)
            a[x + half * index + 1] = value
            kept[x + half * index] = value
            saved[x + half * index] = 0.5 * value
        return carry

    lax.fori_loop(0, half, fill, 0, unroll=4)
    relax(a, b, coarse, saved, 1, True)

    def put(x):
        hi, lo = x // 8, x % 8
        out[hi, 2, lo] = (centre_of(a[x + 1]) + resid[x]) + own[x]
        value = kept[x]
        a[x + 1] = value
        saved[x] = 2.0 * value

    each_x(put)
    for index, base in enumerate((w1, w2)):
        relax(a, b, fine, saved, 2, True)

        def finish(x):
            value = centre_of(a[x + 1])
            out[x // 8, index, x % 8] = value + base[x]
            if index == 1:
                y2[x] = value
            else:
                saved[x] = 2.0 * a[x + 1]

        each_x(finish)
    deal(place[3], out, (out_0, out_1, out_2, out_3), sems)


def end_kernel(
    flags, place, y_c, y_i, y_o, fine, w3, out_0, out_1, out_2, out_3, a, b, saved, out, sems
):
    fl = [flags[k] for k in range(4)]
    clear_ends(a, b)

    def fill(x):
        value = joined(fl, y_c[x], y_i[x], y_o[x])
        a[x + 1] = value
        saved[x] = 2.0 * value

    each_x(fill)
    relax(a, b, fine, saved, 2, True)

    def put(x):
        out[x // 8, x % 8] = centre_of(a[x + 1]) + w3[x]

    each_x(put)
    deal(place[3], out, (out_0, out_1, out_2, out_3), sems)


def split_kernel(parts, place, *refs):
    count = len(parts)
    keep, send = refs[count + 1 : count + 3]
    sems = refs[-1]
    kept = pl.multiple_of(place[4], 2 * ROWS)
    sent = pl.multiple_of(place[5], 2 * ROWS)
    copies = []
    at = 0
    for field, (first, number) in zip(refs, parts):
        for start, target in ((kept, keep), (sent, send)):
            copies.append(
                pltpu.make_async_copy(
                    field.at[pl.ds(first, number), :, pl.ds(start, 2 * ROWS)],
                    target.at[pl.ds(at, number)],
                    sems.at[len(copies)],
                )
            )
        at += number
    together(copies)


def split_four_kernel(place, forcing, guess, after, p_0, p_1, p_2, p_3, sems):
    copies = []
    for index, target in enumerate((p_0, p_1, p_2, p_3)):
        row = pl.multiple_of(jnp.bitwise_xor(place[9], index) * ROWS, ROWS)
        for source, first, at, number in ((forcing, 2, 0, 2), (guess, 0, 2, 1)):
            copies.append(
                pltpu.make_async_copy(
                    source.at[pl.ds(first, number), :, pl.ds(row, ROWS)],
                    target.at[pl.ds(at, number)],
                    sems.at[len(copies)],
                )
            )
    together(copies)


def gather_four_kernel(place, p_0, p_1, p_2, p_3, after, late, own, sems):
    copies = []
    for index, piece in enumerate((p_0, p_1, p_2, p_3)):
        at = pl.multiple_of(jnp.bitwise_xor(place[3], index) * 8, 8)
        for source, target in (
            (piece.at[pl.ds(0, 2)], late.at[:, pl.ds(at, 8)]),
            (piece.at[2], own.at[pl.ds(at, 8)]),
        ):
            copies.append(pltpu.make_async_copy(source, target, sems.at[len(copies)]))
    together(copies)


def split_state_kernel(place, start, guess, keep, send, sems):
    kept = pl.multiple_of(place[4], 2 * ROWS)
    sent = pl.multiple_of(place[5], 2 * ROWS)

    def move(field):
        together(
            [
                pltpu.make_async_copy(field.at[:, pl.ds(at, 2 * ROWS)], target, sems.at[index])
                for index, (at, target) in enumerate(((kept, keep), (sent, send)))
            ]
        )

    @pl.when(place[6] == 1)
    def _():
        move(start)

    @pl.when(place[6] == 0)
    def _():
        move(guess)


def merge_kernel(place, keep, across, state_keep, state_across, out, sems):
    together(
        [
            pltpu.make_async_copy(keep, out.at[0, pl.ds(0, 3)], sems.at[0]),
            pltpu.make_async_copy(across, out.at[1, pl.ds(0, 3)], sems.at[1]),
            pltpu.make_async_copy(state_keep, out.at[0, 3], sems.at[2]),
            pltpu.make_async_copy(state_across, out.at[1, 3], sems.at[3]),
        ]
    )


def gather_kernel(place, mine, other, centre, inner, sems):
    copies = []
    for index, piece in enumerate((mine.at[0], other.at[0], mine.at[1], other.at[1])):
        at = pl.multiple_of(jnp.bitwise_xor(place[3], index) * 8, 8)
        for which, target in ((7, centre), (8, inner)):
            row = pl.multiple_of(place[which], ROWS)
            copies.append(
                pltpu.make_async_copy(
                    piece.at[:, :, pl.ds(row, ROWS)], target.at[:, pl.ds(at, 8)], sems.at[len(copies)]
                )
            )
    together(copies)


def result_kernel(place, *refs):
    first, second, out, sems = refs[:4], refs[4:8], refs[8], refs[9]
    copies = []
    for index in range(4):
        row = pl.multiple_of(jnp.bitwise_xor(place[9], index) * ROWS, ROWS)
        for source, target in (
            (first[index].at[pl.ds(0, 2)], out.at[pl.ds(0, 2), :, pl.ds(row, ROWS)]),
            (second[index], out.at[2, :, pl.ds(row, ROWS)]),
            (first[index].at[2], out.at[3, :, pl.ds(row, ROWS)]),
        ):
            copies.append(pltpu.make_async_copy(source, target, sems.at[len(copies)]))
    together(copies)


def placing(kernel, outs, copies, place, *args):
    specs = [pl.BlockSpec(memory_space=pltpu.SMEM)]
    specs += [pl.BlockSpec(memory_space=pl.ANY)] * len(args)
    return pl.pallas_call(
        kernel,
        out_shape=[jax.ShapeDtypeStruct(shape, F32) for shape in outs],
        in_specs=specs,
        out_specs=[pl.BlockSpec(memory_space=pltpu.VMEM)] * len(outs),
        scratch_shapes=[pltpu.SemaphoreType.DMA((copies,))],
        compiler_params=pltpu.CompilerParams(vmem_limit_bytes=48 * 2**20),
    )(place, *args)


def call(kernel, outs, width, args, smem, extra=(), placed=()):
    scratch = [
        pltpu.VMEM((NX + 2, EXT, width), F32),
        pltpu.VMEM((NX + 2, EXT, width), F32),
        pltpu.VMEM((NX, EXT, width), F32),
    ]
    specs = [
        pl.BlockSpec(memory_space=pltpu.SMEM if index in smem else pltpu.VMEM)
        for index in range(len(args))
    ]
    return pl.pallas_call(
        kernel,
        out_shape=[jax.ShapeDtypeStruct(shape, F32) for shape in outs],
        in_specs=specs,
        out_specs=[
            pl.BlockSpec(memory_space=pl.ANY if index in placed else pltpu.VMEM)
            for index in range(len(outs))
        ],
        scratch_shapes=scratch + list(extra),
        compiler_params=pltpu.CompilerParams(vmem_limit_bytes=48 * 2**20),
    )(*args)


def on_device(start, guess, forcing, absorb):
    tm = lax.axis_index("tm")
    sx = lax.axis_index("sx")
    sy = lax.axis_index("sy")
    turned = sy % 2 == 1
    local = jnp.where(turned, (sx + 2) % 4, sx)
    block = 4 * sy + local
    even = block % 2 == 0
    inner_low = jnp.logical_not(even)
    outer_low = jnp.logical_and(even, block > 0)
    inner_high = even
    outer_high = jnp.logical_and(jnp.logical_not(even), block < 15)
    gate = tm >= GROUP
    flags = jnp.stack([inner_low, outer_low, inner_high, outer_high, gate, tm >= 3 * GROUP]).astype(F32)
    part = tm % GROUP
    half = jnp.where(turned, 1 - sx // 2, sx // 2)
    core = sx % 2
    place = jnp.stack(
        [
            (MARGIN - PART * part) % NZ,
            PART * part - MARGIN,
            ROWS * block - ROWS,
            sx,
            2 * ROWS * half,
            2 * ROWS * (1 - half),
            jnp.where(tm == 15, 1, 0),
            ROWS * core,
            ROWS * (1 - core),
            local,
        ]
    ).astype(jnp.int32)

    def beside(value, step):
        return lax.ppermute(value, "sx", [(i, i ^ step) for i in range(4)])

    def later(value, step):
        pairs = [(4 * c + i, 4 * ((c + 1) % 16) + (i ^ step)) for c in range(16) for i in range(4)]
        return lax.ppermute(value, ("tm", "sx"), pairs)

    def outer(value):
        return lax.ppermute(value, ("sx", "sy"), OFF_CHIP)

    triple = (3, 8, 2 * ROWS, NZ)
    single = (8, 2 * ROWS, NZ)

    field = (NX, ROWS, NZ)
    state_keep, state_send = placing(split_state_kernel, [single] * 2, 2, place, start, guess[0])
    keep, send = placing(
        functools.partial(split_kernel, ((0, 1), (0, 2))), [triple] * 2, 4, place, absorb[None], forcing, place
    )
    state_keep, state_send = later(state_keep, 0), later(state_send, 2)
    (merged,) = placing(
        merge_kernel, [(2, 4, 8, 2 * ROWS, NZ)], 4, place,
        keep, beside(send, 2), state_keep, state_send
    )
    early, early_i = placing(
        gather_kernel, [(4, *field)] * 2, 8, place, merged, beside(merged, 1)
    )
    early_o = outer(early)
    late = placing(split_four_kernel, [(3, 8, ROWS, NZ)] * 4, 8, place, forcing, guess, state_send)
    late = [late[0]] + [beside(late[step], step) for step in (1, 2, 3)]

    late, guess_b = placing(gather_four_kernel, [(2, *field), field], 8, place, *late, early_o)
    late_i, late_o = both_sides(late)
    w1, w2, fine, coarse, window = call(
        begin_kernel,
        [field, field, (NX, EXT, NZ), (NX, EXT, NZ), (NX, EXT, WINDOW)],
        NZ,
        (flags, early, early_i, early_o, place),
        (0, 4),
    )
    w2_i, w2_o = both_sides(w2)
    w3, resid, chunks = call(
        resid_kernel,
        [field, field, (GROUP, NX, ROWS, WINDOW)],
        NZ,
        (flags, w2, w2_i, w2_o, late, late_i, late_o, guess_b, fine),
        (0,),
    )
    groups = [[GROUP * g + j for j in range(GROUP)] for g in range(4)]
    held = lax.all_to_all(chunks, "tm", 0, 0, axis_index_groups=groups)
    held_i, held_o = both_sides(held[: GROUP - 1])
    plane = (NX, ROWS, WINDOW)
    (state,) = call(
        functools.partial(chain_kernel, True, False), [plane], WINDOW,
        (flags, held, held_i, held_o, window), (0,),
    )
    def hop(value, steps):
        return lax.ppermute(value, "tm", [(c, (c + GROUP * steps) % 16) for c in range(16)])

    def chain(value, last, shape):
        value_i, value_o = both_sides(value)
        return call(
            functools.partial(chain_kernel, False, last), [shape], WINDOW,
            (flags, held, held_i, held_o, window, value, value_i, value_o), (0,),
        )[0]

    def power(value):
        value_i, value_o = both_sides(value)
        return call(power_kernel, [plane], WINDOW, (flags, value, value_i, value_o, window), (0,))[0]

    ahead = hop(state, -1)
    state = hop(state, 1)
    ahead = power(ahead)
    state = hop(chain(state, False, plane), 1)
    state = state + flags[5] * power(ahead)
    state = chain(state, True, (GROUP, NX // 2, ROWS, WINDOW))
    error = lax.all_to_all(state, "tm", 0, 0, axis_index_groups=groups)
    error_i, error_o = both_sides(error)
    piece = (3, 8, ROWS, NZ)
    *first, y2 = call(
        correct_kernel,
        [piece] * 4 + [field],
        NZ,
        (flags, place, error, error_i, error_o, fine, coarse, guess_b, resid, w1, w2),
        (0, 1),
        (
            pltpu.VMEM((NX, EXT, NZ), F32),
            pltpu.VMEM((4, *piece), F32),
            pltpu.SemaphoreType.DMA((4,)),
        ),
        range(4),
    )
    y2_i, y2_o = both_sides(y2)
    first = first[:1] + [beside(first[step], step) for step in (1, 2, 3)]
    last = call(
        end_kernel, [piece[1:]] * 4, NZ, (flags, place, y2, y2_i, y2_o, fine, w3), (0, 1),
        (pltpu.VMEM((4, *piece[1:]), F32), pltpu.SemaphoreType.DMA((4,))), range(4),
    )
    last = [last[0]] + [beside(last[step], step) for step in (1, 2, 3)]
    (out,) = placing(result_kernel, [(4, 8, 4 * ROWS, NZ)], 12, place, *first, *last)
    return out


def solution(mesh):
    placed = (
        P("sx", "sy", None),
        P("tm", "sx", "sy", None),
        P("tm", "sx", "sy", None),
        P("sx", "sy", None),
    )
    return jax.shard_map(
        on_device, mesh=mesh, in_specs=placed, out_specs=P("tm", "sx", "sy", None), check_vma=False
    )
```

```python
import functools
import jax
import jax.numpy as jnp
from jax import lax
from jax.experimental import pallas as pl
from jax.experimental.pallas import tpu as pltpu
from jax.sharding import PartitionSpec as P

NX = 32
ROWS = 8
NZ = 256
EXT = 3 * ROWS
PART = 64
MARGIN = 32
WINDOW = PART + 2 * MARGIN
GROUP = 4
F32 = jnp.float32
WX = 2.0
WY = 1.6
WZ = 1.4


def device_of(block):
    sy, local = divmod(block % 16, 4)
    return (local ^ (2 * (sy & 1))) * 4 + sy


def block_swap(first):
    pairs = []
    for block in range(16):
        other = block + 1 if (block - first) % 2 == 0 else block - 1
        pairs.append((device_of(block), device_of(other % 16)))
    return pairs


IN_CHIP = block_swap(0)
OFF_CHIP = block_swap(1)


def both_sides(value):
    axes = ("sx", "sy")
    return lax.ppermute(value, axes, IN_CHIP), lax.ppermute(value, axes, OFF_CHIP)


def sweep(source, target, hinv, saved, closed):
    width = source.shape[2]
    rows = source.shape[1]
    lane = lax.broadcasted_iota(jnp.int32, (rows, width), 1)

    def body(x, carry):
        here = source[x + 1]
        low_z = pltpu.roll(here, 1, 1)
        high_z = pltpu.roll(here, width - 1, 1)
        if closed:
            low_z = jnp.where(lane == 0, 0.0, low_z)
            high_z = jnp.where(lane == width - 1, 0.0, high_z)
        low_y = pltpu.roll(here, 1, 0)
        high_y = pltpu.roll(here, rows - 1, 0)
        total = (source[x + 2] + WX * source[x]) + (high_y + WY * low_y) + (high_z + WZ * low_z)
        target[x + 1] = (total + saved[x]) * hinv[x]
        return carry

    lax.fori_loop(0, NX, body, 0, unroll=True)


def clear_ends(*states):
    for state in states:
        blank = jnp.zeros(state.shape[1:], F32)
        state[0] = blank
        state[NX + 1] = blank


def joined(flags, centre, in_chip, off_chip):
    low = in_chip * flags[0] + off_chip * flags[1]
    high = in_chip * flags[2] + off_chip * flags[3]
    return jnp.concatenate([low, centre, high], axis=0)


def each_x(body):
    def step(x, carry):
        body(x)
        return carry

    lax.fori_loop(0, NX, step, 0, unroll=8)


def relax(a, b, hinv, saved, pairs, closed):
    def pair(index, carry):
        sweep(a, b, hinv, saved, closed)
        sweep(b, a, hinv, saved, closed)
        return carry

    lax.fori_loop(0, pairs, pair, 0)


def centre_of(value):
    return value[ROWS : 2 * ROWS]


def coefficient_kernel(flags, place, s_c, s_i, s_o, fine, coarse, window):
    fl = [flags[k] for k in range(4)]
    shift = place[0]
    lane = lax.broadcasted_iota(jnp.int32, (EXT, WINDOW), 1) + place[1]
    inside = jnp.logical_and(lane >= 0, lane < NZ)
    row = lax.broadcasted_iota(jnp.int32, (EXT, NZ), 0) + place[2]
    real = jnp.logical_and(row >= 0, row < 16 * ROWS)

    def fill(x):
        absorb = joined(fl, s_c[x], s_i[x], s_o[x])
        fine[x] = jnp.where(real, 0.5 / (5.0 + absorb), 0.0)
        value = jnp.where(real, 2.0 / (17.0 + 4.0 * absorb), 0.0)
        coarse[x] = value
        window[x] = jnp.where(inside, pltpu.roll(value, shift, 1)[:, :WINDOW], 0.0)

    each_x(fill)


def begin_kernel(flags, s_c, s_i, s_o, fine, w1, w2, a, b, saved):
    fl = [flags[k] for k in range(4)]
    clear_ends(a, b)

    def source(index, x):
        return joined(fl, s_c[index, x], s_i[index, x], s_o[index, x])

    def fill(x):
        value = source(2, x)
        a[x + 1] = value
        saved[x] = 2.0 * (value + source(0, x))

    each_x(fill)
    relax(a, b, fine, saved, 2, True)

    def turn(x):
        value = a[x + 1]
        w1[x] = centre_of(value)
        saved[x] = 2.0 * (value + source(1, x))

    each_x(turn)
    relax(a, b, fine, saved, 2, True)

    def put(x):
        w2[x] = centre_of(a[x + 1])

    each_x(put)


def pull_kernel(flags, s_c, s_i, s_o, coarse, before, pulled, a, b, saved):
    fl = [flags[k] for k in range(4)]
    gate = flags[6]
    clear_ends(a, b)

    def fill(x):
        value = joined(fl, s_c[2, x], s_i[2, x], s_o[2, x])
        before[x] = value
        a[x + 1] = value
        saved[x] = 0.5 * value

    each_x(fill)
    relax(a, b, coarse, saved, 1, True)

    def put(x):
        pulled[x] = gate * centre_of(a[x + 1])

    each_x(put)


def resid_kernel(flags, v_c, v_i, v_o, s_c, s_i, s_o, pulled, fine, w3, w4, chunks, a, b, saved):
    fl = [flags[k] for k in range(4)]
    clear_ends(a, b)

    def source(index, x):
        return joined(fl, s_c[index, x], s_i[index, x], s_o[index, x])

    def fill(x):
        value = joined(fl, v_c[x], v_i[x], v_o[x])
        a[x + 1] = value
        saved[x] = 2.0 * (value + source(0, x))

    each_x(fill)
    relax(a, b, fine, saved, 2, True)

    def turn(x):
        value = a[x + 1]
        w3[x] = centre_of(value)
        saved[x] = 2.0 * (value + source(1, x))

    each_x(turn)
    relax(a, b, fine, saved, 2, True)
    lane = lax.broadcasted_iota(jnp.int32, (ROWS, WINDOW), 1)

    def split(x):
        value = centre_of(a[x + 1])
        w4[x] = value
        value = value - pulled[x]
        for part in range(GROUP):
            start = PART * part - MARGIN
            turned = pltpu.roll(value, (-start) % NZ, 1)[:, :WINDOW]
            if part == 0:
                turned = jnp.where(lane < MARGIN, 0.0, turned)
            if part == GROUP - 1:
                turned = jnp.where(lane >= WINDOW - MARGIN, 0.0, turned)
            chunks[part, x] = turned

    each_x(split)


def chain_kernel(first, last, flags, r_c, r_i, r_o, hinv, *refs):
    if first:
        out, a, b, saved = refs
    else:
        e_c, e_i, e_o, out, a, b, saved = refs
    fl = [flags[k] for k in range(4)]
    clear_ends(a, b)
    lane = lax.broadcasted_iota(jnp.int32, (ROWS, WINDOW), 1)

    def added(step, x):
        if step < GROUP - 1:
            return joined(fl, r_c[step, x], r_i[step, x], r_o[step, x])
        blank = jnp.zeros((ROWS, WINDOW), F32)
        return jnp.concatenate([blank, r_c[step, x], blank], axis=0)

    def fill(x):
        value = added(0, x) if first else flags[4] * joined(fl, e_c[x], e_i[x], e_o[x])
        a[x + 1] = value
        saved[x] = 0.5 * value

    each_x(fill)

    def pack(step):
        def put(x, carry):
            low = pltpu.roll(centre_of(a[x + 1]), WINDOW - MARGIN, 1)
            high = pltpu.roll(centre_of(a[x + 1 + NX // 2]), MARGIN, 1)
            out[step, x] = jnp.where(lane < PART, low, high)
            return carry

        lax.fori_loop(0, NX // 2, put, 0, unroll=8)

    for step in range(1 if first else 0, GROUP):
        if last:
            pack(step)
            if step == GROUP - 1:
                return
        relax(a, b, hinv, saved, 1, False)

        def add(x):
            value = a[x + 1] + added(step, x)
            a[x + 1] = value
            saved[x] = 0.5 * value

        each_x(add)

    def put_all(x):
        out[x] = centre_of(a[x + 1])

    each_x(put_all)


def power_kernel(flags, e_c, e_i, e_o, hinv, out, a, b, saved):
    fl = [flags[k] for k in range(4)]
    clear_ends(a, b)

    def fill(x):
        value = joined(fl, e_c[x], e_i[x], e_o[x])
        a[x + 1] = value
        saved[x] = 0.5 * value

    each_x(fill)
    for step in range(GROUP):
        relax(a, b, hinv, saved, 1, False)
        if step < GROUP - 1:

            def again(x):
                saved[x] = 0.5 * a[x + 1]

            each_x(again)

    def put(x):
        out[x] = centre_of(a[x + 1])

    each_x(put)


def unpacked(packed, x, lane):
    p = [packed[part, x] for part in range(GROUP)]
    low = lane < PART
    first = jnp.concatenate(
        [jnp.where(low, p[0], pltpu.roll(p[1], PART, 1)), jnp.where(low, p[2], pltpu.roll(p[3], PART, 1))],
        axis=1,
    )
    second = jnp.concatenate(
        [jnp.where(low, pltpu.roll(p[0], PART, 1), p[1]), jnp.where(low, pltpu.roll(p[2], PART, 1), p[3])],
        axis=1,
    )
    return first, second


def together(copies):
    for copy in copies:
        copy.start()
    for copy in copies:
        copy.wait()


def deal(sx, source, targets, sems):
    together(
        [
            pltpu.make_async_copy(source.at[jnp.bitwise_xor(sx, index)], target, sems.at[index])
            for index, target in enumerate(targets)
        ]
    )


def onward_kernel(flags, d_c, d_i, d_o, fine, before, d, y1, y2, a, b, saved):
    fl = [flags[k] for k in range(4)]
    clear_ends(a, b)
    lane = lax.broadcasted_iota(jnp.int32, (ROWS, WINDOW), 1)
    half = NX // 2

    def fill(x, carry):
        for index, values in enumerate(
            zip(unpacked(d_c, x, lane), unpacked(d_i, x, lane), unpacked(d_o, x, lane))
        ):
            value = flags[6] * (joined(fl, *values) - before[x + half * index])
            a[x + half * index + 1] = value
            d[x + half * index] = value
            saved[x + half * index] = 2.0 * value
        return carry

    lax.fori_loop(0, half, fill, 0, unroll=4)
    relax(a, b, fine, saved, 2, True)

    def turn(x):
        value = a[x + 1]
        y1[x] = centre_of(value)
        saved[x] = 2.0 * value

    each_x(turn)
    relax(a, b, fine, saved, 2, True)

    def finish(x):
        y2[x] = centre_of(a[x + 1])

    each_x(finish)


def correct_kernel(
    place, d, coarse, w1, w2, w4, y1, y2, out_0, out_1, out_2, out_3, a, b, saved, out, sems
):
    clear_ends(a, b)

    def fill(x):
        value = d[x]
        a[x + 1] = value
        saved[x] = 0.5 * value

    each_x(fill)
    relax(a, b, coarse, saved, 1, True)

    def put(x):
        hi, lo = x // 8, x % 8
        out[hi, 0, lo] = y1[x] + w1[x]
        out[hi, 1, lo] = y2[x] + w2[x]
        out[hi, 2, lo] = centre_of(a[x + 1]) + w4[x]

    each_x(put)
    deal(place[3], out, (out_0, out_1, out_2, out_3), sems)


def end_kernel(
    flags, place, y_c, y_i, y_o, fine, w3, out_0, out_1, out_2, out_3, a, b, saved, out, sems
):
    fl = [flags[k] for k in range(4)]
    clear_ends(a, b)

    def fill(x):
        value = joined(fl, y_c[x], y_i[x], y_o[x])
        a[x + 1] = value
        saved[x] = 2.0 * value

    each_x(fill)
    relax(a, b, fine, saved, 2, True)

    def put(x):
        out[x // 8, x % 8] = centre_of(a[x + 1]) + w3[x]

    each_x(put)
    deal(place[3], out, (out_0, out_1, out_2, out_3), sems)


def split_kernel(place, start, guess, absorb, forcing, state_k, state_s, keep, send_a, send_f, sems):
    kept = pl.ds(pl.multiple_of(place[4], 2 * ROWS), 2 * ROWS)
    sent = pl.ds(pl.multiple_of(place[5], 2 * ROWS), 2 * ROWS)
    pair = pl.ds(0, 2)
    moves = [
        (absorb.at[:, kept], keep.at[0]),
        (absorb.at[:, sent], send_a),
        (forcing.at[pair, :, kept], keep.at[pl.ds(1, 2)]),
        (forcing.at[pair, :, sent], send_f),
    ]

    def move(field):
        every = moves + [(field.at[:, kept], state_k), (field.at[:, sent], state_s)]
        together(
            [
                pltpu.make_async_copy(source, target, sems.at[index])
                for index, (source, target) in enumerate(every)
            ]
        )

    @pl.when(place[6] == 1)
    def _():
        move(start)

    @pl.when(place[6] == 0)
    def _():
        move(guess.at[0])


def split_four_kernel(place, forcing, after, p_0, p_1, p_2, p_3, sems):
    copies = []
    for index, target in enumerate((p_0, p_1, p_2, p_3)):
        row = pl.multiple_of(jnp.bitwise_xor(place[9], index) * ROWS, ROWS)
        copies.append(
            pltpu.make_async_copy(
                forcing.at[pl.ds(2, 2), :, pl.ds(row, ROWS)], target, sems.at[index]
            )
        )
    together(copies)


def gather_four_kernel(place, p_0, p_1, p_2, p_3, after, late, sems):
    copies = []
    for index, piece in enumerate((p_0, p_1, p_2, p_3)):
        at = pl.multiple_of(jnp.bitwise_xor(place[3], index) * 8, 8)
        copies.append(pltpu.make_async_copy(piece, late.at[:, pl.ds(at, 8)], sems.at[index]))
    together(copies)


def merge_kernel(place, keep, across_a, across_f, state_keep, state_across, out, sems):
    moves = (
        (keep, out.at[0, pl.ds(0, 3)]),
        (across_a, out.at[1, 0]),
        (across_f, out.at[1, pl.ds(1, 2)]),
        (state_keep, out.at[0, 3]),
        (state_across, out.at[1, 3]),
    )
    together(
        [
            pltpu.make_async_copy(source, target, sems.at[index])
            for index, (source, target) in enumerate(moves)
        ]
    )


def gather_kernel(place, mine, other, centre_a, centre, inner_a, inner, sems):
    copies = []
    for index, piece in enumerate((mine.at[0], other.at[0], mine.at[1], other.at[1])):
        at = pl.ds(pl.multiple_of(jnp.bitwise_xor(place[3], index) * 8, 8), 8)
        for which, one, three in ((7, centre_a, centre), (8, inner_a, inner)):
            rows = pl.ds(pl.multiple_of(place[which], ROWS), ROWS)
            for source, target in (
                (piece.at[0, :, rows], one.at[at]),
                (piece.at[pl.ds(1, 3), :, rows], three.at[:, at]),
            ):
                copies.append(pltpu.make_async_copy(source, target, sems.at[len(copies)]))
    together(copies)


def result_kernel(place, *refs):
    first, second, out, sems = refs[:4], refs[4:8], refs[8], refs[9]
    copies = []
    for index in range(4):
        row = pl.multiple_of(jnp.bitwise_xor(place[9], index) * ROWS, ROWS)
        for source, target in (
            (first[index].at[pl.ds(0, 2)], out.at[pl.ds(0, 2), :, pl.ds(row, ROWS)]),
            (second[index], out.at[2, :, pl.ds(row, ROWS)]),
            (first[index].at[2], out.at[3, :, pl.ds(row, ROWS)]),
        ):
            copies.append(pltpu.make_async_copy(source, target, sems.at[len(copies)]))
    together(copies)


def placing(kernel, outs, copies, place, *args, grant=48):
    specs = [pl.BlockSpec(memory_space=pltpu.SMEM)]
    specs += [pl.BlockSpec(memory_space=pl.ANY)] * len(args)
    return pl.pallas_call(
        kernel,
        out_shape=[jax.ShapeDtypeStruct(shape, F32) for shape in outs],
        in_specs=specs,
        out_specs=[pl.BlockSpec(memory_space=pltpu.VMEM)] * len(outs),
        scratch_shapes=[pltpu.SemaphoreType.DMA((copies,))],
        compiler_params=pltpu.CompilerParams(vmem_limit_bytes=grant * 2**20),
    )(place, *args)


def call(kernel, outs, width, args, smem, extra=(), placed=(), state=True, loose=()):
    scratch = [
        pltpu.VMEM((NX + 2, EXT, width), F32),
        pltpu.VMEM((NX + 2, EXT, width), F32),
        pltpu.VMEM((NX, EXT, width), F32),
    ]
    specs = [
        pl.BlockSpec(
            memory_space=pltpu.SMEM if index in smem else pl.ANY if index in loose else pltpu.VMEM
        )
        for index in range(len(args))
    ]
    return pl.pallas_call(
        kernel,
        out_shape=[jax.ShapeDtypeStruct(shape, F32) for shape in outs],
        in_specs=specs,
        out_specs=[
            pl.BlockSpec(memory_space=pl.ANY if index in placed else pltpu.VMEM)
            for index in range(len(outs))
        ],
        scratch_shapes=(scratch if state else []) + list(extra),
        compiler_params=pltpu.CompilerParams(vmem_limit_bytes=48 * 2**20),
    )(*args)


def on_device(start, guess, forcing, absorb):
    tm = lax.axis_index("tm")
    sx = lax.axis_index("sx")
    sy = lax.axis_index("sy")
    turned = sy % 2 == 1
    local = jnp.where(turned, (sx + 2) % 4, sx)
    block = 4 * sy + local
    even = block % 2 == 0
    inner_low = jnp.logical_not(even)
    outer_low = jnp.logical_and(even, block > 0)
    inner_high = even
    outer_high = jnp.logical_and(jnp.logical_not(even), block < 15)
    gate = tm >= GROUP
    flags = jnp.stack([inner_low, outer_low, inner_high, outer_high, gate, tm >= 3 * GROUP, tm > 0]).astype(F32)
    part = tm % GROUP
    half = jnp.where(turned, 1 - sx // 2, sx // 2)
    core = sx % 2
    place = jnp.stack(
        [
            (MARGIN - PART * part) % NZ,
            PART * part - MARGIN,
            ROWS * block - ROWS,
            sx,
            2 * ROWS * half,
            2 * ROWS * (1 - half),
            jnp.where(tm == 15, 1, 0),
            ROWS * core,
            ROWS * (1 - core),
            local,
        ]
    ).astype(jnp.int32)

    def beside(value, step):
        return lax.ppermute(value, "sx", [(i, i ^ step) for i in range(4)])

    def later(value, step):
        pairs = [(4 * c + i, 4 * ((c + 1) % 16) + (i ^ step)) for c in range(16) for i in range(4)]
        return lax.ppermute(value, ("tm", "sx"), pairs)

    def outer(value):
        return lax.ppermute(value, ("sx", "sy"), OFF_CHIP)

    def other_chip(value):
        pairs = []
        for c in range(16):
            for i in range(4):
                pairs.append((4 * c + i, 4 * ((c - 4 if i < 2 else c + 4) % 16) + (i ^ 2)))
        return lax.ppermute(value, ("tm", "sx"), pairs)

    def outer_other_chip(value):
        pairs = []
        for c in range(16):
            for here, there in OFF_CHIP:
                step = 4 * (here // 8 - there // 8) if here % 4 == there % 4 else 0
                pairs.append((16 * c + here, 16 * ((c + step) % 16) + there))
        return lax.ppermute(value, ("tm", "sx", "sy"), pairs)

    field = (NX, ROWS, NZ)
    single = (8, 2 * ROWS, NZ)
    state_keep, state_send, keep, send_a, send_f = placing(
        split_kernel, [single, single, (3, *single), single, (2, *single)], 6, place,
        start, guess, absorb, forcing
    )
    state_keep, state_send = later(state_keep, 0), later(state_send, 2)
    (merged,) = placing(
        merge_kernel, [(2, 4, *single)], 5, place,
        keep, other_chip(send_a), beside(send_f, 2), state_keep, state_send
    )
    early_a, early, early_a_i, early_i = placing(
        gather_kernel, [field, (3, *field)] * 2, 16, place, merged, beside(merged, 1)
    )
    early_a_o = outer_other_chip(early_a)
    early_o = outer(early)
    late = placing(split_four_kernel, [(2, 8, ROWS, NZ)] * 4, 4, place, forcing, state_send)
    late = [late[0]] + [beside(late[step], step) for step in (1, 2, 3)]

    fine, coarse, window = call(
        coefficient_kernel, [(NX, EXT, NZ), (NX, EXT, NZ), (NX, EXT, WINDOW)], NZ,
        (flags, place, early_a, early_a_i, early_a_o), (0, 1), state=False
    )
    w1, w2 = call(
        begin_kernel, [field, field], NZ, (flags, early, early_i, early_o, fine), (0,)
    )
    w2_i, w2_o = both_sides(w2)
    (late,) = placing(gather_four_kernel, [(2, *field)], 4, place, *late, w2)
    late_i, late_o = both_sides(late)
    before, pulled = call(
        pull_kernel, [(NX, EXT, NZ), field], NZ, (flags, early, early_i, early_o, coarse), (0,)
    )
    w3, w4, chunks = call(
        resid_kernel,
        [field, field, (GROUP, NX, ROWS, WINDOW)],
        NZ,
        (flags, w2, w2_i, w2_o, late, late_i, late_o, pulled, fine),
        (0,),
    )
    groups = [[GROUP * g + j for j in range(GROUP)] for g in range(4)]
    held = lax.all_to_all(chunks, "tm", 0, 0, axis_index_groups=groups)
    held_i, held_o = both_sides(held[: GROUP - 1])
    plane = (NX, ROWS, WINDOW)
    (state,) = call(
        functools.partial(chain_kernel, True, False), [plane], WINDOW,
        (flags, held, held_i, held_o, window), (0,),
    )
    def hop(value, steps):
        return lax.ppermute(value, "tm", [(c, (c + GROUP * steps) % 16) for c in range(16)])

    def chain(value, last, shape):
        value_i, value_o = both_sides(value)
        return call(
            functools.partial(chain_kernel, False, last), [shape], WINDOW,
            (flags, held, held_i, held_o, window, value, value_i, value_o), (0,),
        )[0]

    def power(value):
        value_i, value_o = both_sides(value)
        return call(power_kernel, [plane], WINDOW, (flags, value, value_i, value_o, window), (0,))[0]

    ahead = hop(state, -1)
    state = hop(state, 1)
    ahead = power(ahead)
    state = hop(chain(state, False, plane), 1)
    state = state + flags[5] * power(ahead)
    state = chain(state, True, (GROUP, NX // 2, ROWS, WINDOW))
    error = lax.all_to_all(state, "tm", 0, 0, axis_index_groups=groups)
    error_i, error_o = both_sides(error)
    piece = (3, 8, ROWS, NZ)
    d, y1, y2 = call(
        onward_kernel, [(NX, EXT, NZ), field, field], NZ,
        (flags, error, error_i, error_o, fine, before), (0,)
    )
    y2_i, y2_o = both_sides(y2)
    first = call(
        correct_kernel, [piece] * 4, NZ,
        (place, d, coarse, w1, w2, w4, y1, y2), (0,),
        (pltpu.VMEM((4, *piece), F32), pltpu.SemaphoreType.DMA((4,))), range(4),
    )
    first = [first[0]] + [beside(first[step], step) for step in (1, 2, 3)]
    last = call(
        end_kernel, [piece[1:]] * 4, NZ, (flags, place, y2, y2_i, y2_o, fine, w3), (0, 1),
        (pltpu.VMEM((4, *piece[1:]), F32), pltpu.SemaphoreType.DMA((4,))), range(4),
    )
    last = [last[0]] + [beside(last[step], step) for step in (1, 2, 3)]
    (out,) = placing(result_kernel, [(4, 8, 4 * ROWS, NZ)], 12, place, *first, *last)
    return out


def solution(mesh):
    placed = (
        P("sx", "sy", None),
        P("tm", "sx", "sy", None),
        P("tm", "sx", "sy", None),
        P("sx", "sy", None),
    )
    return jax.shard_map(
        on_device, mesh=mesh, in_specs=placed, out_specs=P("tm", "sx", "sy", None), check_vma=False
    )
```

```python
import functools
import jax
import jax.numpy as jnp
from jax import lax
from jax.experimental import pallas as pl
from jax.experimental.pallas import tpu as pltpu
from jax.sharding import PartitionSpec as P

NX = 32
ROWS = 8
NZ = 256
EXT = 3 * ROWS
PART = 64
MARGIN = 32
WINDOW = PART + 2 * MARGIN
GROUP = 4
F32 = jnp.float32
WX = 2.0
WY = 1.6
WZ = 1.4


def device_of(block):
    sy, local = divmod(block % 16, 4)
    return (local ^ (2 * (sy & 1))) * 4 + sy


def block_swap(first):
    pairs = []
    for block in range(16):
        other = block + 1 if (block - first) % 2 == 0 else block - 1
        pairs.append((device_of(block), device_of(other % 16)))
    return pairs


IN_CHIP = block_swap(0)
OFF_CHIP = block_swap(1)


def both_sides(value):
    axes = ("sx", "sy")
    return lax.ppermute(value, axes, IN_CHIP), lax.ppermute(value, axes, OFF_CHIP)


def sweep(source, target, hinv, saved, closed):
    width = source.shape[2]
    rows = source.shape[1]
    lane = lax.broadcasted_iota(jnp.int32, (rows, width), 1)

    def body(x, carry):
        here = source[x + 1]
        low_z = pltpu.roll(here, 1, 1)
        high_z = pltpu.roll(here, width - 1, 1)
        if closed:
            low_z = jnp.where(lane == 0, 0.0, low_z)
            high_z = jnp.where(lane == width - 1, 0.0, high_z)
        low_y = pltpu.roll(here, 1, 0)
        high_y = pltpu.roll(here, rows - 1, 0)
        total = (source[x + 2] + WX * source[x]) + (high_y + WY * low_y) + (high_z + WZ * low_z)
        target[x + 1] = (total + saved[x]) * hinv[x]
        return carry

    lax.fori_loop(0, NX, body, 0, unroll=True)


def clear_ends(*states):
    for state in states:
        blank = jnp.zeros(state.shape[1:], F32)
        state[0] = blank
        state[NX + 1] = blank


def joined(flags, centre, in_chip, off_chip):
    low = in_chip * flags[0] + off_chip * flags[1]
    high = in_chip * flags[2] + off_chip * flags[3]
    return jnp.concatenate([low, centre, high], axis=0)


def each_x(body):
    def step(x, carry):
        body(x)
        return carry

    lax.fori_loop(0, NX, step, 0, unroll=8)


def relax(a, b, hinv, saved, pairs, closed):
    def pair(index, carry):
        sweep(a, b, hinv, saved, closed)
        sweep(b, a, hinv, saved, closed)
        return carry

    lax.fori_loop(0, pairs, pair, 0)


def centre_of(value):
    return value[ROWS : 2 * ROWS]


def coefficient_kernel(flags, place, s_c, s_i, s_o, fine, coarse, window):
    fl = [flags[k] for k in range(4)]
    shift = place[0]
    lane = lax.broadcasted_iota(jnp.int32, (EXT, WINDOW), 1) + place[1]
    inside = jnp.logical_and(lane >= 0, lane < NZ)
    row = lax.broadcasted_iota(jnp.int32, (EXT, NZ), 0) + place[2]
    real = jnp.logical_and(row >= 0, row < 16 * ROWS)

    def fill(x):
        absorb = joined(fl, s_c[x], s_i[x], s_o[x])
        fine[x] = jnp.where(real, 0.5 / (5.0 + absorb), 0.0)
        value = jnp.where(real, 2.0 / (17.0 + 4.0 * absorb), 0.0)
        coarse[x] = value
        window[x] = jnp.where(inside, pltpu.roll(value, shift, 1)[:, :WINDOW], 0.0)

    each_x(fill)


def begin_kernel(flags, s_c, s_i, s_o, fine, w1, w2, a, b, saved):
    fl = [flags[k] for k in range(4)]
    clear_ends(a, b)

    def source(index, x):
        return joined(fl, s_c[index, x], s_i[index, x], s_o[index, x])

    def fill(x):
        value = source(2, x)
        a[x + 1] = value
        saved[x] = 2.0 * (value + source(0, x))

    each_x(fill)
    relax(a, b, fine, saved, 2, True)

    def turn(x):
        value = a[x + 1]
        w1[x] = centre_of(value)
        saved[x] = 2.0 * (value + source(1, x))

    each_x(turn)
    relax(a, b, fine, saved, 2, True)

    def put(x):
        w2[x] = centre_of(a[x + 1])

    each_x(put)


def pull_kernel(flags, s_c, s_i, s_o, coarse, before, pulled, a, b, saved):
    fl = [flags[k] for k in range(4)]
    gate = flags[6]
    clear_ends(a, b)

    def fill(x):
        value = joined(fl, s_c[2, x], s_i[2, x], s_o[2, x])
        before[x] = value
        a[x + 1] = value
        saved[x] = 0.5 * value

    each_x(fill)
    relax(a, b, coarse, saved, 1, True)

    def put(x):
        pulled[x] = gate * centre_of(a[x + 1])

    each_x(put)


def resid_kernel(flags, v_c, v_i, v_o, s_c, s_i, s_o, pulled, fine, w3, w4, chunks, a, b, saved):
    fl = [flags[k] for k in range(4)]
    clear_ends(a, b)

    def source(index, x):
        return joined(fl, s_c[index, x], s_i[index, x], s_o[index, x])

    def fill(x):
        value = joined(fl, v_c[x], v_i[x], v_o[x])
        a[x + 1] = value
        saved[x] = 2.0 * (value + source(0, x))

    each_x(fill)
    relax(a, b, fine, saved, 2, True)

    def turn(x):
        value = a[x + 1]
        w3[x] = centre_of(value)
        saved[x] = 2.0 * (value + source(1, x))

    each_x(turn)
    relax(a, b, fine, saved, 2, True)
    lane = lax.broadcasted_iota(jnp.int32, (ROWS, WINDOW), 1)

    def split(x):
        value = centre_of(a[x + 1])
        w4[x] = value
        value = value - pulled[x]
        for part in range(GROUP):
            start = PART * part - MARGIN
            turned = pltpu.roll(value, (-start) % NZ, 1)[:, :WINDOW]
            if part == 0:
                turned = jnp.where(lane < MARGIN, 0.0, turned)
            if part == GROUP - 1:
                turned = jnp.where(lane >= WINDOW - MARGIN, 0.0, turned)
            chunks[part, x] = turned

    each_x(split)


def chain_kernel(first, last, flags, r_c, r_i, r_o, hinv, *refs):
    if first:
        out, a, b, saved = refs
    else:
        e_c, e_i, e_o, out, a, b, saved = refs
    fl = [flags[k] for k in range(4)]
    clear_ends(a, b)
    lane = lax.broadcasted_iota(jnp.int32, (ROWS, WINDOW), 1)

    def added(step, x):
        if step < GROUP - 1:
            return joined(fl, r_c[step, x], r_i[step, x], r_o[step, x])
        blank = jnp.zeros((ROWS, WINDOW), F32)
        return jnp.concatenate([blank, r_c[step, x], blank], axis=0)

    def fill(x):
        value = added(0, x) if first else flags[4] * joined(fl, e_c[x], e_i[x], e_o[x])
        a[x + 1] = value
        saved[x] = 0.5 * value

    each_x(fill)

    def pack(step):
        def put(x, carry):
            low = pltpu.roll(centre_of(a[x + 1]), WINDOW - MARGIN, 1)
            high = pltpu.roll(centre_of(a[x + 1 + NX // 2]), MARGIN, 1)
            out[step, x] = jnp.where(lane < PART, low, high)
            return carry

        lax.fori_loop(0, NX // 2, put, 0, unroll=8)

    for step in range(1 if first else 0, GROUP):
        if last:
            pack(step)
            if step == GROUP - 1:
                return
        relax(a, b, hinv, saved, 1, False)

        def add(x):
            value = a[x + 1] + added(step, x)
            a[x + 1] = value
            saved[x] = 0.5 * value

        each_x(add)

    def put_all(x):
        out[x] = centre_of(a[x + 1])

    each_x(put_all)


def power_kernel(flags, e_c, e_i, e_o, hinv, out, a, b, saved):
    fl = [flags[k] for k in range(4)]
    clear_ends(a, b)

    def fill(x):
        value = joined(fl, e_c[x], e_i[x], e_o[x])
        a[x + 1] = value
        saved[x] = 0.5 * value

    each_x(fill)
    for step in range(GROUP):
        relax(a, b, hinv, saved, 1, False)
        if step < GROUP - 1:

            def again(x):
                saved[x] = 0.5 * a[x + 1]

            each_x(again)

    def put(x):
        out[x] = centre_of(a[x + 1])

    each_x(put)


def unpacked(packed, x, lane):
    p = [packed[part, x] for part in range(GROUP)]
    low = lane < PART
    first = jnp.concatenate(
        [jnp.where(low, p[0], pltpu.roll(p[1], PART, 1)), jnp.where(low, p[2], pltpu.roll(p[3], PART, 1))],
        axis=1,
    )
    second = jnp.concatenate(
        [jnp.where(low, pltpu.roll(p[0], PART, 1), p[1]), jnp.where(low, pltpu.roll(p[2], PART, 1), p[3])],
        axis=1,
    )
    return first, second


def together(copies):
    for copy in copies:
        copy.start()
    for copy in copies:
        copy.wait()


def deal(sx, source, targets, sems):
    together(
        [
            pltpu.make_async_copy(source.at[jnp.bitwise_xor(sx, index)], target, sems.at[index])
            for index, target in enumerate(targets)
        ]
    )


def onward_kernel(flags, d_c, d_i, d_o, fine, before, d, y1, y2, a, b, saved):
    fl = [flags[k] for k in range(4)]
    clear_ends(a, b)
    lane = lax.broadcasted_iota(jnp.int32, (ROWS, WINDOW), 1)
    half = NX // 2

    def fill(x, carry):
        for index, values in enumerate(
            zip(unpacked(d_c, x, lane), unpacked(d_i, x, lane), unpacked(d_o, x, lane))
        ):
            value = flags[6] * (joined(fl, *values) - before[x + half * index])
            a[x + half * index + 1] = value
            d[x + half * index] = value
            saved[x + half * index] = 2.0 * value
        return carry

    lax.fori_loop(0, half, fill, 0, unroll=4)
    relax(a, b, fine, saved, 2, True)

    def turn(x):
        value = a[x + 1]
        y1[x] = centre_of(value)
        saved[x] = 2.0 * value

    each_x(turn)
    relax(a, b, fine, saved, 2, True)

    def finish(x):
        y2[x] = centre_of(a[x + 1])

    each_x(finish)


def correct_kernel(
    place, d, coarse, w1, w2, w4, y1, y2, out_0, out_1, out_2, out_3, a, b, saved, out, sems
):
    clear_ends(a, b)

    def fill(x):
        value = d[x]
        a[x + 1] = value
        saved[x] = 0.5 * value

    each_x(fill)
    relax(a, b, coarse, saved, 1, True)

    def put(x):
        hi, lo = x // 8, x % 8
        out[hi, 0, lo] = y1[x] + w1[x]
        out[hi, 1, lo] = y2[x] + w2[x]
        out[hi, 2, lo] = centre_of(a[x + 1]) + w4[x]

    each_x(put)
    deal(place[3], out, (out_0, out_1, out_2, out_3), sems)


def end_kernel(
    flags, place, y_c, y_i, y_o, fine, w3, out_0, out_1, out_2, out_3, a, b, saved, out, sems
):
    fl = [flags[k] for k in range(4)]
    clear_ends(a, b)

    def fill(x):
        value = joined(fl, y_c[x], y_i[x], y_o[x])
        a[x + 1] = value
        saved[x] = 2.0 * value

    each_x(fill)
    relax(a, b, fine, saved, 2, True)

    def put(x):
        out[x // 8, x % 8] = centre_of(a[x + 1]) + w3[x]

    each_x(put)
    deal(place[3], out, (out_0, out_1, out_2, out_3), sems)


def rows_of(local):
    return pl.ds(pl.multiple_of(local * ROWS, ROWS), ROWS)


def copied(moves, sems):
    together(
        [
            pltpu.make_async_copy(source, target, sems.at[index])
            for index, (source, target) in enumerate(moves)
        ]
    )


def split_state_kernel(place, start, guess, start_p, guess_p, here, across, sems):
    def move(own, other):
        copied(
            [
                (field.at[:, rows_of(jnp.bitwise_xor(place[4], step))], target.at[index])
                for index, field in enumerate((own, other))
                for step, target in ((0, here), (2, across))
            ],
            sems,
        )

    @pl.when(place[5] == 1)
    def _():
        move(start, start_p)

    @pl.when(place[5] == 0)
    def _():
        move(guess.at[0], guess_p.at[0])


def split_kernel(place, absorb, forcing, absorb_p, forcing_p, send_a, send_f, sems):
    rows = rows_of(jnp.bitwise_xor(place[4], 2))
    first = pl.ds(0, 2)
    copied(
        (
            (absorb.at[:, rows], send_a.at[0]),
            (absorb_p.at[:, rows], send_a.at[1]),
            (forcing.at[first, :, rows], send_f.at[0]),
            (forcing_p.at[first, :, rows], send_f.at[1]),
        ),
        sems,
    )


def split_late_kernel(place, forcing, forcing_p, after, send, sems):
    rows = rows_of(jnp.bitwise_xor(place[4], 2))
    last = pl.ds(2, 2)
    copied(
        ((forcing.at[last, :, rows], send.at[0]), (forcing_p.at[last, :, rows], send.at[1])), sems
    )


def octet(place, index):
    return pl.ds(pl.multiple_of(jnp.bitwise_xor(place[3], index) * 8, 8), 8)


def gather_absorb_kernel(place, absorb, absorb_p, across, centre, sems):
    rows = rows_of(place[4])
    sources = (absorb.at[:, rows], absorb_p.at[:, rows], across.at[0], across.at[1])
    copied([(source, centre.at[octet(place, index)]) for index, source in enumerate(sources)], sems)


def gather_kernel(place, forcing, forcing_p, across, here, beyond, after, centre, sems):
    rows = rows_of(place[4])
    first = pl.ds(0, 2)
    sources = (
        (forcing.at[first, :, rows], here.at[0]),
        (forcing_p.at[first, :, rows], here.at[1]),
        (across.at[0], beyond.at[0]),
        (across.at[1], beyond.at[1]),
    )
    moves = []
    for index, (two, state) in enumerate(sources):
        at = octet(place, index)
        moves += [(two, centre.at[first, at]), (state, centre.at[2, at])]
    copied(moves, sems)


def gather_late_kernel(place, forcing, forcing_p, across, after, centre, sems):
    rows = rows_of(place[4])
    last = pl.ds(2, 2)
    sources = (
        forcing.at[last, :, rows], forcing_p.at[last, :, rows], across.at[0], across.at[1]
    )
    copied(
        [(source, centre.at[:, octet(place, index)]) for index, source in enumerate(sources)], sems
    )


def result_kernel(place, *refs):
    first, second, out, sems = refs[:4], refs[4:8], refs[8], refs[9]
    copies = []
    for index in range(4):
        row = pl.multiple_of(jnp.bitwise_xor(place[4], index) * ROWS, ROWS)
        for source, target in (
            (first[index].at[pl.ds(0, 2)], out.at[pl.ds(0, 2), :, pl.ds(row, ROWS)]),
            (second[index], out.at[2, :, pl.ds(row, ROWS)]),
            (first[index].at[2], out.at[3, :, pl.ds(row, ROWS)]),
        ):
            copies.append(pltpu.make_async_copy(source, target, sems.at[len(copies)]))
    together(copies)


def placing(kernel, outs, copies, place, *args, grant=48):
    specs = [pl.BlockSpec(memory_space=pltpu.SMEM)]
    specs += [pl.BlockSpec(memory_space=pl.ANY)] * len(args)
    return pl.pallas_call(
        kernel,
        out_shape=[jax.ShapeDtypeStruct(shape, F32) for shape in outs],
        in_specs=specs,
        out_specs=[pl.BlockSpec(memory_space=pltpu.VMEM)] * len(outs),
        scratch_shapes=[pltpu.SemaphoreType.DMA((copies,))],
        compiler_params=pltpu.CompilerParams(vmem_limit_bytes=grant * 2**20),
    )(place, *args)


def call(kernel, outs, width, args, smem, extra=(), placed=(), state=True, loose=()):
    scratch = [
        pltpu.VMEM((NX + 2, EXT, width), F32),
        pltpu.VMEM((NX + 2, EXT, width), F32),
        pltpu.VMEM((NX, EXT, width), F32),
    ]
    specs = [
        pl.BlockSpec(
            memory_space=pltpu.SMEM if index in smem else pl.ANY if index in loose else pltpu.VMEM
        )
        for index in range(len(args))
    ]
    return pl.pallas_call(
        kernel,
        out_shape=[jax.ShapeDtypeStruct(shape, F32) for shape in outs],
        in_specs=specs,
        out_specs=[
            pl.BlockSpec(memory_space=pl.ANY if index in placed else pltpu.VMEM)
            for index in range(len(outs))
        ],
        scratch_shapes=(scratch if state else []) + list(extra),
        compiler_params=pltpu.CompilerParams(vmem_limit_bytes=48 * 2**20),
    )(*args)


def on_device(start, guess, forcing, absorb):
    tm = lax.axis_index("tm")
    sx = lax.axis_index("sx")
    sy = lax.axis_index("sy")
    turned = sy % 2 == 1
    local = jnp.where(turned, (sx + 2) % 4, sx)
    block = 4 * sy + local
    even = block % 2 == 0
    inner_low = jnp.logical_not(even)
    outer_low = jnp.logical_and(even, block > 0)
    inner_high = even
    outer_high = jnp.logical_and(jnp.logical_not(even), block < 15)
    gate = tm >= GROUP
    flags = jnp.stack([inner_low, outer_low, inner_high, outer_high, gate, tm >= 3 * GROUP, tm > 0]).astype(F32)
    part = tm % GROUP
    place = jnp.stack(
        [
            (MARGIN - PART * part) % NZ,
            PART * part - MARGIN,
            ROWS * block - ROWS,
            sx,
            local,
            jnp.where(tm == 15, 1, 0),
        ]
    ).astype(jnp.int32)

    def beside(value, step):
        return lax.ppermute(value, "sx", [(i, i ^ step) for i in range(4)])

    def later(value, step):
        pairs = [(4 * c + i, 4 * ((c + 1) % 16) + (i ^ step)) for c in range(16) for i in range(4)]
        return lax.ppermute(value, ("tm", "sx"), pairs)

    def outer(value):
        return lax.ppermute(value, ("sx", "sy"), OFF_CHIP)

    def other_chip(value):
        pairs = []
        for c in range(16):
            for i in range(4):
                pairs.append((4 * c + i, 4 * ((c - 4 if i < 2 else c + 4) % 16) + (i ^ 2)))
        return lax.ppermute(value, ("tm", "sx"), pairs)

    def outer_other_chip(value):
        pairs = []
        for c in range(16):
            for here, there in OFF_CHIP:
                step = 4 * (here // 8 - there // 8) if here % 4 == there % 4 else 0
                pairs.append((16 * c + here, 16 * ((c + step) % 16) + there))
        return lax.ppermute(value, ("tm", "sx", "sy"), pairs)

    field = (NX, ROWS, NZ)
    piece = (8, ROWS, NZ)
    guess_p, start_p = beside(guess, 1), beside(start, 1)
    here, beyond = placing(
        split_state_kernel, [(2, *piece)] * 2, 4, place, start, guess, start_p, guess_p
    )
    here, beyond = later(here, 0), later(beyond, 2)
    absorb_p, forcing_p = beside(absorb, 1), beside(forcing, 1)
    send_a, send_f = placing(
        split_kernel, [(2, *piece), (2, 2, *piece)], 4, place, absorb, forcing, absorb_p, forcing_p
    )
    across_a, across_f = other_chip(send_a), beside(send_f, 2)
    (early_a,) = placing(
        gather_absorb_kernel, [field], 4, place, absorb, absorb_p, across_a
    )
    (early,) = placing(
        gather_kernel, [(3, *field)], 8, place, forcing, forcing_p, across_f, here, beyond, across_a
    )
    early_a_i, early_a_o = beside(early_a, 1), outer_other_chip(early_a)
    early_i, early_o = both_sides(early)
    (late,) = placing(split_late_kernel, [(2, 2, *piece)], 2, place, forcing, forcing_p, early)
    late = beside(late, 2)

    fine, coarse, window = call(
        coefficient_kernel, [(NX, EXT, NZ), (NX, EXT, NZ), (NX, EXT, WINDOW)], NZ,
        (flags, place, early_a, early_a_i, early_a_o), (0, 1), state=False
    )
    w1, w2 = call(
        begin_kernel, [field, field], NZ, (flags, early, early_i, early_o, fine), (0,)
    )
    w2_i, w2_o = both_sides(w2)
    (late,) = placing(gather_late_kernel, [(2, *field)], 4, place, forcing, forcing_p, late, w2)
    late_i, late_o = both_sides(late)
    before, pulled = call(
        pull_kernel, [(NX, EXT, NZ), field], NZ, (flags, early, early_i, early_o, coarse), (0,)
    )
    w3, w4, chunks = call(
        resid_kernel,
        [field, field, (GROUP, NX, ROWS, WINDOW)],
        NZ,
        (flags, w2, w2_i, w2_o, late, late_i, late_o, pulled, fine),
        (0,),
    )
    groups = [[GROUP * g + j for j in range(GROUP)] for g in range(4)]
    held = lax.all_to_all(chunks, "tm", 0, 0, axis_index_groups=groups)
    held_i, held_o = both_sides(held[: GROUP - 1])
    plane = (NX, ROWS, WINDOW)
    (state,) = call(
        functools.partial(chain_kernel, True, False), [plane], WINDOW,
        (flags, held, held_i, held_o, window), (0,),
    )
    def hop(value, steps):
        return lax.ppermute(value, "tm", [(c, (c + GROUP * steps) % 16) for c in range(16)])

    def chain(value, last, shape):
        value_i, value_o = both_sides(value)
        return call(
            functools.partial(chain_kernel, False, last), [shape], WINDOW,
            (flags, held, held_i, held_o, window, value, value_i, value_o), (0,),
        )[0]

    def power(value):
        value_i, value_o = both_sides(value)
        return call(power_kernel, [plane], WINDOW, (flags, value, value_i, value_o, window), (0,))[0]

    ahead = hop(state, -1)
    state = hop(state, 1)
    ahead = power(ahead)
    state = hop(chain(state, False, plane), 1)
    state = state + flags[5] * power(ahead)
    state = chain(state, True, (GROUP, NX // 2, ROWS, WINDOW))
    error = lax.all_to_all(state, "tm", 0, 0, axis_index_groups=groups)
    error_i, error_o = both_sides(error)
    piece = (3, 8, ROWS, NZ)
    d, y1, y2 = call(
        onward_kernel, [(NX, EXT, NZ), field, field], NZ,
        (flags, error, error_i, error_o, fine, before), (0,)
    )
    y2_i, y2_o = both_sides(y2)
    first = call(
        correct_kernel, [piece] * 4, NZ,
        (place, d, coarse, w1, w2, w4, y1, y2), (0,),
        (pltpu.VMEM((4, *piece), F32), pltpu.SemaphoreType.DMA((4,))), range(4),
    )
    first = [first[0]] + [beside(first[step], step) for step in (1, 2, 3)]
    last = call(
        end_kernel, [piece[1:]] * 4, NZ, (flags, place, y2, y2_i, y2_o, fine, w3), (0, 1),
        (pltpu.VMEM((4, *piece[1:]), F32), pltpu.SemaphoreType.DMA((4,))), range(4),
    )
    last = [last[0]] + [beside(last[step], step) for step in (1, 2, 3)]
    (out,) = placing(result_kernel, [(4, 8, 4 * ROWS, NZ)], 12, place, *first, *last)
    return out


def solution(mesh):
    placed = (
        P("sx", "sy", None),
        P("tm", "sx", "sy", None),
        P("tm", "sx", "sy", None),
        P("sx", "sy", None),
    )
    return jax.shard_map(
        on_device, mesh=mesh, in_specs=placed, out_specs=P("tm", "sx", "sy", None), check_vma=False
    )
```

```python
import functools
import jax
import jax.numpy as jnp
from jax import lax
from jax.experimental import pallas as pl
from jax.experimental.pallas import tpu as pltpu
from jax.sharding import PartitionSpec as P

NX = 32
ROWS = 8
NZ = 256
EXT = 3 * ROWS
PART = 64
MARGIN = 32
WINDOW = PART + 2 * MARGIN
GROUP = 4
F32 = jnp.float32
WX = 2.0
WY = 1.6
WZ = 1.4


def device_of(block):
    sy, local = divmod(block % 16, 4)
    return (local ^ (2 * (sy & 1))) * 4 + sy


def block_swap(first):
    pairs = []
    for block in range(16):
        other = block + 1 if (block - first) % 2 == 0 else block - 1
        pairs.append((device_of(block), device_of(other % 16)))
    return pairs


IN_CHIP = block_swap(0)
OFF_CHIP = block_swap(1)


def both_sides(value):
    axes = ("sx", "sy")
    return lax.ppermute(value, axes, IN_CHIP), lax.ppermute(value, axes, OFF_CHIP)


def sweep(source, target, hinv, saved, closed):
    width = source.shape[2]
    rows = source.shape[1]
    lane = lax.broadcasted_iota(jnp.int32, (rows, width), 1)

    def body(x, carry):
        here = source[x + 1]
        low_z = pltpu.roll(here, 1, 1)
        high_z = pltpu.roll(here, width - 1, 1)
        if closed:
            low_z = jnp.where(lane == 0, 0.0, low_z)
            high_z = jnp.where(lane == width - 1, 0.0, high_z)
        low_y = pltpu.roll(here, 1, 0)
        high_y = pltpu.roll(here, rows - 1, 0)
        total = (source[x + 2] + WX * source[x]) + (high_y + WY * low_y) + (high_z + WZ * low_z)
        target[x + 1] = (total + saved[x]) * hinv[x]
        return carry

    lax.fori_loop(0, NX, body, 0, unroll=True)


def clear_ends(*states):
    for state in states:
        blank = jnp.zeros(state.shape[1:], F32)
        state[0] = blank
        state[NX + 1] = blank


def joined(flags, centre, in_chip, off_chip):
    low = in_chip * flags[0] + off_chip * flags[1]
    high = in_chip * flags[2] + off_chip * flags[3]
    return jnp.concatenate([low, centre, high], axis=0)


def each_x(body):
    def step(x, carry):
        body(x)
        return carry

    lax.fori_loop(0, NX, step, 0, unroll=True)


def relax(a, b, hinv, saved, pairs, closed):
    def pair(index, carry):
        sweep(a, b, hinv, saved, closed)
        sweep(b, a, hinv, saved, closed)
        return carry

    lax.fori_loop(0, pairs, pair, 0)


def centre_of(value):
    return value[ROWS : 2 * ROWS]


def coefficient_kernel(flags, place, s_c, s_i, s_o, fine, coarse, window):
    fl = [flags[k] for k in range(4)]
    shift = place[0]
    lane = lax.broadcasted_iota(jnp.int32, (EXT, WINDOW), 1) + place[1]
    inside = jnp.logical_and(lane >= 0, lane < NZ)
    row = lax.broadcasted_iota(jnp.int32, (EXT, NZ), 0) + place[2]
    real = jnp.logical_and(row >= 0, row < 16 * ROWS)

    def fill(x):
        absorb = joined(fl, s_c[x], s_i[x], s_o[x])
        fine[x] = jnp.where(real, 0.5 / (5.0 + absorb), 0.0)
        value = jnp.where(real, 2.0 / (17.0 + 4.0 * absorb), 0.0)
        coarse[x] = value
        window[x] = jnp.where(inside, pltpu.roll(value, shift, 1)[:, :WINDOW], 0.0)

    each_x(fill)


def begin_kernel(flags, s_c, s_i, s_o, fine, w1, w2, a, b, saved):
    fl = [flags[k] for k in range(4)]
    clear_ends(a, b)

    def source(index, x):
        return joined(fl, s_c[index, x], s_i[index, x], s_o[index, x])

    def fill(x):
        value = source(2, x)
        a[x + 1] = value
        saved[x] = 2.0 * (value + source(0, x))

    each_x(fill)
    relax(a, b, fine, saved, 2, True)

    def turn(x):
        value = a[x + 1]
        w1[x] = centre_of(value)
        saved[x] = 2.0 * (value + source(1, x))

    each_x(turn)
    relax(a, b, fine, saved, 2, True)

    def put(x):
        w2[x] = centre_of(a[x + 1])

    each_x(put)


def pull_kernel(flags, s_c, s_i, s_o, coarse, before, pulled, a, b, saved):
    fl = [flags[k] for k in range(4)]
    gate = flags[6]
    clear_ends(a, b)

    def fill(x):
        value = joined(fl, s_c[2, x], s_i[2, x], s_o[2, x])
        before[x] = value
        a[x + 1] = value
        saved[x] = 0.5 * value

    each_x(fill)
    relax(a, b, coarse, saved, 1, True)

    def put(x):
        pulled[x] = gate * centre_of(a[x + 1])

    each_x(put)


def resid_kernel(flags, v_c, v_i, v_o, s_c, s_i, s_o, pulled, fine, w3, w4, chunks, a, b, saved):
    fl = [flags[k] for k in range(4)]
    clear_ends(a, b)

    def source(index, x):
        return joined(fl, s_c[index, x], s_i[index, x], s_o[index, x])

    def fill(x):
        value = joined(fl, v_c[x], v_i[x], v_o[x])
        a[x + 1] = value
        saved[x] = 2.0 * (value + source(0, x))

    each_x(fill)
    relax(a, b, fine, saved, 2, True)

    def turn(x):
        value = a[x + 1]
        w3[x] = centre_of(value)
        saved[x] = 2.0 * (value + source(1, x))

    each_x(turn)
    relax(a, b, fine, saved, 2, True)
    lane = lax.broadcasted_iota(jnp.int32, (ROWS, WINDOW), 1)

    def split(x):
        value = centre_of(a[x + 1])
        w4[x] = value
        value = value - pulled[x]
        for part in range(GROUP):
            start = PART * part - MARGIN
            turned = pltpu.roll(value, (-start) % NZ, 1)[:, :WINDOW]
            if part == 0:
                turned = jnp.where(lane < MARGIN, 0.0, turned)
            if part == GROUP - 1:
                turned = jnp.where(lane >= WINDOW - MARGIN, 0.0, turned)
            chunks[part, x] = turned

    each_x(split)


def chain_kernel(first, last, flags, r_c, r_i, r_o, hinv, *refs):
    if first:
        out, a, b, saved = refs
    else:
        e_c, e_i, e_o, out, a, b, saved = refs
    fl = [flags[k] for k in range(4)]
    clear_ends(a, b)
    lane = lax.broadcasted_iota(jnp.int32, (ROWS, WINDOW), 1)

    def added(step, x):
        if step < GROUP - 1:
            return joined(fl, r_c[step, x], r_i[step, x], r_o[step, x])
        blank = jnp.zeros((ROWS, WINDOW), F32)
        return jnp.concatenate([blank, r_c[step, x], blank], axis=0)

    def fill(x):
        value = added(0, x) if first else flags[4] * joined(fl, e_c[x], e_i[x], e_o[x])
        a[x + 1] = value
        saved[x] = 0.5 * value

    each_x(fill)

    def pack(step):
        def put(x, carry):
            low = pltpu.roll(centre_of(a[x + 1]), WINDOW - MARGIN, 1)
            high = pltpu.roll(centre_of(a[x + 1 + NX // 2]), MARGIN, 1)
            out[step, x] = jnp.where(lane < PART, low, high)
            return carry

        lax.fori_loop(0, NX // 2, put, 0, unroll=True)

    for step in range(1 if first else 0, GROUP):
        if last:
            pack(step)
            if step == GROUP - 1:
                return
        relax(a, b, hinv, saved, 1, False)

        def add(x):
            value = a[x + 1] + added(step, x)
            a[x + 1] = value
            saved[x] = 0.5 * value

        each_x(add)

    def put_all(x):
        out[x] = centre_of(a[x + 1])

    each_x(put_all)


def power_kernel(gated, flags, e_c, e_i, e_o, hinv, out, a, b, saved):
    fl = [flags[k] for k in range(4)]
    clear_ends(a, b)

    def fill(x):
        value = joined(fl, e_c[x], e_i[x], e_o[x])
        a[x + 1] = value
        saved[x] = 0.5 * value

    each_x(fill)
    for step in range(GROUP):
        relax(a, b, hinv, saved, 1, False)
        if step < GROUP - 1:

            def again(x):
                saved[x] = 0.5 * a[x + 1]

            each_x(again)

    def put(x):
        value = centre_of(a[x + 1])
        out[x] = flags[5] * value if gated else value

    each_x(put)


def unpacked(packed, x, lane):
    p = [packed[part, x] for part in range(GROUP)]
    low = lane < PART
    first = jnp.concatenate(
        [jnp.where(low, p[0], pltpu.roll(p[1], PART, 1)), jnp.where(low, p[2], pltpu.roll(p[3], PART, 1))],
        axis=1,
    )
    second = jnp.concatenate(
        [jnp.where(low, pltpu.roll(p[0], PART, 1), p[1]), jnp.where(low, pltpu.roll(p[2], PART, 1), p[3])],
        axis=1,
    )
    return first, second


def together(copies):
    for copy in copies:
        copy.start()
    for copy in copies:
        copy.wait()


def deal(sx, source, targets, sems):
    together(
        [
            pltpu.make_async_copy(source.at[jnp.bitwise_xor(sx, index)], target, sems.at[index])
            for index, target in enumerate(targets)
        ]
    )


def onward_kernel(flags, d_c, d_i, d_o, fine, before, d, y1, y2, a, b, saved):
    fl = [flags[k] for k in range(4)]
    clear_ends(a, b)
    lane = lax.broadcasted_iota(jnp.int32, (ROWS, WINDOW), 1)
    half = NX // 2

    def fill(x, carry):
        for index, values in enumerate(
            zip(unpacked(d_c, x, lane), unpacked(d_i, x, lane), unpacked(d_o, x, lane))
        ):
            value = flags[6] * (joined(fl, *values) - before[x + half * index])
            a[x + half * index + 1] = value
            d[x + half * index] = value
            saved[x + half * index] = 2.0 * value
        return carry

    lax.fori_loop(0, half, fill, 0, unroll=True)
    relax(a, b, fine, saved, 2, True)

    def turn(x):
        value = a[x + 1]
        y1[x] = centre_of(value)
        saved[x] = 2.0 * value

    each_x(turn)
    relax(a, b, fine, saved, 2, True)

    def finish(x):
        y2[x] = centre_of(a[x + 1])

    each_x(finish)


def correct_kernel(
    place, d, coarse, w1, w2, w4, y1, y2, out_0, out_1, out_2, out_3, a, b, saved, out, sems
):
    clear_ends(a, b)

    def fill(x):
        value = d[x]
        a[x + 1] = value
        saved[x] = 0.5 * value

    each_x(fill)
    relax(a, b, coarse, saved, 1, True)

    def put(x):
        hi, lo = x // 8, x % 8
        out[hi, 0, lo] = y1[x] + w1[x]
        out[hi, 1, lo] = y2[x] + w2[x]
        out[hi, 2, lo] = centre_of(a[x + 1]) + w4[x]

    each_x(put)
    deal(place[3], out, (out_0, out_1, out_2, out_3), sems)


def end_kernel(
    flags, place, y_c, y_i, y_o, fine, w3, out_0, out_1, out_2, out_3, a, b, saved, out, sems
):
    fl = [flags[k] for k in range(4)]
    clear_ends(a, b)

    def fill(x):
        value = joined(fl, y_c[x], y_i[x], y_o[x])
        a[x + 1] = value
        saved[x] = 2.0 * value

    each_x(fill)
    relax(a, b, fine, saved, 2, True)

    def put(x):
        out[x // 8, x % 8] = centre_of(a[x + 1]) + w3[x]

    each_x(put)
    deal(place[3], out, (out_0, out_1, out_2, out_3), sems)


def rows_of(local):
    return pl.ds(pl.multiple_of(local * ROWS, ROWS), ROWS)


def copied(moves, sems):
    together(
        [
            pltpu.make_async_copy(source, target, sems.at[index])
            for index, (source, target) in enumerate(moves)
        ]
    )


def split_state_kernel(place, start, guess, start_p, guess_p, here, across, sems):
    def move(own, other):
        copied(
            [
                (field.at[:, rows_of(jnp.bitwise_xor(place[4], step))], target.at[index])
                for index, field in enumerate((own, other))
                for step, target in ((0, here), (2, across))
            ],
            sems,
        )

    @pl.when(place[5] == 1)
    def _():
        move(start, start_p)

    @pl.when(place[5] == 0)
    def _():
        move(guess.at[0], guess_p.at[0])


def split_kernel(place, absorb, forcing, absorb_p, forcing_p, send_a, send_f, sems):
    rows = rows_of(jnp.bitwise_xor(place[4], 2))
    first = pl.ds(0, 2)
    copied(
        (
            (absorb.at[:, rows], send_a.at[0]),
            (absorb_p.at[:, rows], send_a.at[1]),
            (forcing.at[first, :, rows], send_f.at[0]),
            (forcing_p.at[first, :, rows], send_f.at[1]),
        ),
        sems,
    )


def split_late_kernel(place, forcing, forcing_p, after, send, sems):
    rows = rows_of(jnp.bitwise_xor(place[4], 2))
    last = pl.ds(2, 2)
    copied(
        ((forcing.at[last, :, rows], send.at[0]), (forcing_p.at[last, :, rows], send.at[1])), sems
    )


def octet(place, index):
    return pl.ds(pl.multiple_of(jnp.bitwise_xor(place[3], index) * 8, 8), 8)


def gather_absorb_kernel(place, absorb, absorb_p, across, centre, sems):
    rows = rows_of(place[4])
    sources = (absorb.at[:, rows], absorb_p.at[:, rows], across.at[0], across.at[1])
    copied([(source, centre.at[octet(place, index)]) for index, source in enumerate(sources)], sems)


def gather_kernel(place, forcing, forcing_p, across, here, beyond, after, centre, sems):
    rows = rows_of(place[4])
    first = pl.ds(0, 2)
    sources = (
        (forcing.at[first, :, rows], here.at[0]),
        (forcing_p.at[first, :, rows], here.at[1]),
        (across.at[0], beyond.at[0]),
        (across.at[1], beyond.at[1]),
    )
    moves = []
    for index, (two, state) in enumerate(sources):
        at = octet(place, index)
        moves += [(two, centre.at[first, at]), (state, centre.at[2, at])]
    copied(moves, sems)


def gather_late_kernel(place, forcing, forcing_p, across, after, centre, sems):
    rows = rows_of(place[4])
    last = pl.ds(2, 2)
    sources = (
        forcing.at[last, :, rows], forcing_p.at[last, :, rows], across.at[0], across.at[1]
    )
    copied(
        [(source, centre.at[:, octet(place, index)]) for index, source in enumerate(sources)], sems
    )


def result_kernel(place, *refs):
    first, second, out, sems = refs[:4], refs[4:8], refs[8], refs[9]
    copies = []
    for index in range(4):
        row = pl.multiple_of(jnp.bitwise_xor(place[4], index) * ROWS, ROWS)
        for source, target in (
            (first[index].at[pl.ds(0, 2)], out.at[pl.ds(0, 2), :, pl.ds(row, ROWS)]),
            (second[index], out.at[2, :, pl.ds(row, ROWS)]),
            (first[index].at[2], out.at[3, :, pl.ds(row, ROWS)]),
        ):
            copies.append(pltpu.make_async_copy(source, target, sems.at[len(copies)]))
    together(copies)


def placing(kernel, outs, copies, place, *args, grant=48):
    specs = [pl.BlockSpec(memory_space=pltpu.SMEM)]
    specs += [pl.BlockSpec(memory_space=pl.ANY)] * len(args)
    return pl.pallas_call(
        kernel,
        out_shape=[jax.ShapeDtypeStruct(shape, F32) for shape in outs],
        in_specs=specs,
        out_specs=[pl.BlockSpec(memory_space=pltpu.VMEM)] * len(outs),
        scratch_shapes=[pltpu.SemaphoreType.DMA((copies,))],
        compiler_params=pltpu.CompilerParams(vmem_limit_bytes=grant * 2**20),
    )(place, *args)


def call(kernel, outs, width, args, smem, extra=(), placed=(), state=True, loose=()):
    scratch = [
        pltpu.VMEM((NX + 2, EXT, width), F32),
        pltpu.VMEM((NX + 2, EXT, width), F32),
        pltpu.VMEM((NX, EXT, width), F32),
    ]
    specs = [
        pl.BlockSpec(
            memory_space=pltpu.SMEM if index in smem else pl.ANY if index in loose else pltpu.VMEM
        )
        for index in range(len(args))
    ]
    return pl.pallas_call(
        kernel,
        out_shape=[jax.ShapeDtypeStruct(shape, F32) for shape in outs],
        in_specs=specs,
        out_specs=[
            pl.BlockSpec(memory_space=pl.ANY if index in placed else pltpu.VMEM)
            for index in range(len(outs))
        ],
        scratch_shapes=(scratch if state else []) + list(extra),
        compiler_params=pltpu.CompilerParams(vmem_limit_bytes=48 * 2**20),
    )(*args)


def on_device(start, guess, forcing, absorb):
    tm = lax.axis_index("tm")
    sx = lax.axis_index("sx")
    sy = lax.axis_index("sy")
    turned = sy % 2 == 1
    local = jnp.where(turned, (sx + 2) % 4, sx)
    block = 4 * sy + local
    even = block % 2 == 0
    inner_low = jnp.logical_not(even)
    outer_low = jnp.logical_and(even, block > 0)
    inner_high = even
    outer_high = jnp.logical_and(jnp.logical_not(even), block < 15)
    gate = tm >= GROUP
    flags = jnp.stack([inner_low, outer_low, inner_high, outer_high, gate, tm >= 3 * GROUP, tm > 0]).astype(F32)
    part = tm % GROUP
    place = jnp.stack(
        [
            (MARGIN - PART * part) % NZ,
            PART * part - MARGIN,
            ROWS * block - ROWS,
            sx,
            local,
            jnp.where(tm == 15, 1, 0),
        ]
    ).astype(jnp.int32)

    def beside(value, step):
        return lax.ppermute(value, "sx", [(i, i ^ step) for i in range(4)])

    def later(value, step):
        pairs = [(4 * c + i, 4 * ((c + 1) % 16) + (i ^ step)) for c in range(16) for i in range(4)]
        return lax.ppermute(value, ("tm", "sx"), pairs)

    def outer(value):
        return lax.ppermute(value, ("sx", "sy"), OFF_CHIP)

    def other_chip(value):
        pairs = []
        for c in range(16):
            for i in range(4):
                pairs.append((4 * c + i, 4 * ((c - 4 if i < 2 else c + 4) % 16) + (i ^ 2)))
        return lax.ppermute(value, ("tm", "sx"), pairs)

    def outer_other_chip(value):
        pairs = []
        for c in range(16):
            for here, there in OFF_CHIP:
                step = 4 * (here // 8 - there // 8) if here % 4 == there % 4 else 0
                pairs.append((16 * c + here, 16 * ((c + step) % 16) + there))
        return lax.ppermute(value, ("tm", "sx", "sy"), pairs)

    field = (NX, ROWS, NZ)
    piece = (8, ROWS, NZ)
    guess_p, start_p = beside(guess, 1), beside(start, 1)
    here, beyond = placing(
        split_state_kernel, [(2, *piece)] * 2, 4, place, start, guess, start_p, guess_p
    )
    here, beyond = later(here, 0), later(beyond, 2)
    absorb_p, forcing_p = beside(absorb, 1), beside(forcing, 1)
    send_a, send_f = placing(
        split_kernel, [(2, *piece), (2, 2, *piece)], 4, place, absorb, forcing, absorb_p, forcing_p
    )
    across_a, across_f = other_chip(send_a), beside(send_f, 2)
    (early_a,) = placing(
        gather_absorb_kernel, [field], 4, place, absorb, absorb_p, across_a
    )
    (early,) = placing(
        gather_kernel, [(3, *field)], 8, place, forcing, forcing_p, across_f, here, beyond, across_a
    )
    early_a_i, early_a_o = beside(early_a, 1), outer_other_chip(early_a)
    early_i, early_o = both_sides(early)
    (late,) = placing(split_late_kernel, [(2, 2, *piece)], 2, place, forcing, forcing_p, early)
    late = beside(late, 2)

    fine, coarse, window = call(
        coefficient_kernel, [(NX, EXT, NZ), (NX, EXT, NZ), (NX, EXT, WINDOW)], NZ,
        (flags, place, early_a, early_a_i, early_a_o), (0, 1), state=False
    )
    w1, w2 = call(
        begin_kernel, [field, field], NZ, (flags, early, early_i, early_o, fine), (0,)
    )
    w2_i, w2_o = both_sides(w2)
    (late,) = placing(gather_late_kernel, [(2, *field)], 4, place, forcing, forcing_p, late, w2)
    late_i, late_o = both_sides(late)
    before, pulled = call(
        pull_kernel, [(NX, EXT, NZ), field], NZ, (flags, early, early_i, early_o, coarse), (0,)
    )
    w3, w4, chunks = call(
        resid_kernel,
        [field, field, (GROUP, NX, ROWS, WINDOW)],
        NZ,
        (flags, w2, w2_i, w2_o, late, late_i, late_o, pulled, fine),
        (0,),
    )
    groups = [[GROUP * g + j for j in range(GROUP)] for g in range(4)]
    held = lax.all_to_all(chunks, "tm", 0, 0, axis_index_groups=groups)
    held_i, held_o = both_sides(held[: GROUP - 1])
    plane = (NX, ROWS, WINDOW)
    (state,) = call(
        functools.partial(chain_kernel, True, False), [plane], WINDOW,
        (flags, held, held_i, held_o, window), (0,),
    )
    def hop(value, steps):
        return lax.ppermute(value, "tm", [(c, (c + GROUP * steps) % 16) for c in range(16)])

    def chain(value, last, shape):
        value_i, value_o = both_sides(value)
        return call(
            functools.partial(chain_kernel, False, last), [shape], WINDOW,
            (flags, held, held_i, held_o, window, value, value_i, value_o), (0,),
        )[0]

    def power(value, gated):
        value_i, value_o = both_sides(value)
        return call(
            functools.partial(power_kernel, gated), [plane], WINDOW,
            (flags, value, value_i, value_o, window), (0,)
        )[0]

    ahead = hop(state, -1)
    state = hop(state, 1)
    ahead = power(ahead, False)
    state = hop(chain(state, False, plane), 1)
    state = state + power(ahead, True)
    state = chain(state, True, (GROUP, NX // 2, ROWS, WINDOW))
    error = lax.all_to_all(state, "tm", 0, 0, axis_index_groups=groups)
    error_i, error_o = both_sides(error)
    piece = (3, 8, ROWS, NZ)
    d, y1, y2 = call(
        onward_kernel, [(NX, EXT, NZ), field, field], NZ,
        (flags, error, error_i, error_o, fine, before), (0,)
    )
    y2_i, y2_o = both_sides(y2)
    first = call(
        correct_kernel, [piece] * 4, NZ,
        (place, d, coarse, w1, w2, w4, y1, y2), (0,),
        (pltpu.VMEM((4, *piece), F32), pltpu.SemaphoreType.DMA((4,))), range(4),
    )
    first = [first[0]] + [beside(first[step], step) for step in (1, 2, 3)]
    last = call(
        end_kernel, [piece[1:]] * 4, NZ, (flags, place, y2, y2_i, y2_o, fine, w3), (0, 1),
        (pltpu.VMEM((4, *piece[1:]), F32), pltpu.SemaphoreType.DMA((4,))), range(4),
    )
    last = [last[0]] + [beside(last[step], step) for step in (1, 2, 3)]
    (out,) = placing(result_kernel, [(4, 8, 4 * ROWS, NZ)], 12, place, *first, *last)
    return out


def solution(mesh):
    placed = (
        P("sx", "sy", None),
        P("tm", "sx", "sy", None),
        P("tm", "sx", "sy", None),
        P("sx", "sy", None),
    )
    return jax.shard_map(
        on_device, mesh=mesh, in_specs=placed, out_specs=P("tm", "sx", "sy", None), check_vma=False
    )
```
